32 devices in a mesh: il: 4 (over y, x), xl: 2 (over core), ta: 4 (over z).
Axes of the slice: x: 2, y: 2, z: 4, core: 2. Of those that a mesh axis runs over, the one named last changes fastest.
Arguments:
- traces: float32 [128, 64, 512], P('il', 'xl', 'ta'), may hold values from -6 to 6
- live: int32 [128, 64], P('il', 'xl'), may hold values 0 or 1
- counts: int32 [4, 2, 8], P('il', None, 'ta'), may hold values from 2 to 4, as said below
- levels: int32 [4], replicated, may hold values from 100 to 1500, as said below
Outputs:
- reconstructed: float32 [128, 64, 512], P('il', 'xl', 'ta')
The draws below stay inside these ranges and needn't reach their ends.
Inputs may be any that keep to these rules, and one draw needn't show every extreme that they name: counts[i, x, 2 t + w] is the iteration count of window w of the block of tile (i, x, t); a value of 4 occurs in every draw. `levels`: non-increasing over the iterations.
All inputs are finite; a program needn't handle non-finite values. No bound on the sum of `live` on one device may be relied on, other than what follows from the above.
Results may differ from the reference program's by a relative error of at most 0.0003.
Values may be sent and summed in bfloat16 or wider, within the bound.
A program may use at most 64 MiB of HBM per device.

```python
import jax
import jax.numpy as jnp
from jax import lax

WIN = 64
WIN_T = 128
WPD = 2
MAXIT = 4
HALO = 16
HALO_T = 32
CORE = 32
CORE_T = 64
NI = 128
NX = 64
NT = 512
N_IL = 4
N_XL = 2
N_TA = 4


def window_plan(key):
    base_key = jax.random.fold_in(key, 11)
    key_pair, key_side, key_heavy = jax.random.split(base_key, 3)
    pair_count = N_XL // 2
    busy_pair = jax.random.randint(key_pair, (N_IL, pair_count, N_TA), 0, 2)
    first_line = (jnp.arange(N_IL)[:, None, None] == 0) & (jnp.arange(pair_count)[None, :, None] == 0) & (jnp.arange(N_TA)[None, None, :] == 0)
    busy_pair = jnp.where(first_line, 1, busy_pair)
    busy_side = jax.random.randint(key_side, (N_IL, pair_count, N_TA), 0, 2)
    parity = jnp.arange(N_XL) % 2
    busy_device = jnp.repeat(busy_pair, 2, axis=1) * (jnp.repeat(busy_side, 2, axis=1) == parity[None, :, None])
    heavy_counts = jax.random.randint(key_heavy, (N_IL, N_XL, N_TA, WPD), MAXIT - 1, MAXIT + 1)
    heavy_counts = jnp.where(jnp.arange(WPD)[None, None, None, :] == 0, MAXIT, heavy_counts)
    light_counts = jnp.full((N_IL, N_XL, N_TA, WPD), 2, jnp.int32)
    chosen = jnp.where(busy_device[:, :, :, None] == 1, heavy_counts, light_counts)
    return chosen.reshape(N_IL, N_XL, N_TA * WPD).astype(jnp.int32)


def draw_counts(key, part):
    return window_plan(key)


def draw_levels(key, part):
    values = jax.random.randint(jax.random.fold_in(key, 5), (MAXIT,), 100, 1501)
    ordered = -jnp.sort(-values)
    steps = jnp.arange(MAXIT)
    ordered = jnp.where(steps == 0, 1500, ordered)
    ordered = jnp.where(steps == MAXIT - 1, 100, ordered)
    return ordered.astype(jnp.int32)


def place_ends(array, stream_key, smallest, high):
    longest = array.shape.index(max(array.shape))
    spots = []
    for shift in (0, 1):
        where = [jax.random.randint(jax.random.fold_in(stream_key, axis), (), 0, length) for axis, length in enumerate(array.shape)]
        where[longest] = (where[longest] + shift) % array.shape[longest]
        spots.append(tuple(where))
    return array.at[spots[0]].set(smallest).at[spots[1]].set(high)


def block_scale(stream_key, dims, cuts, low, top_value):
    loudness = 1.0
    for dim, parts in cuts:
        steps = jax.random.uniform(jax.random.fold_in(jax.random.fold_in(stream_key, 6), dim), (parts,), jnp.float32, low / len(cuts), top_value / len(cuts))
        loudness = loudness * jnp.repeat(jnp.exp(steps), dims[dim] // parts).reshape((-1,) + (1,) * (len(dims) - 1 - dim))
    return loudness


def normal_values(stream_key, dims, deviation, reach, cuts=(), held_as=jnp.bfloat16):
    level = block_scale(stream_key, dims, cuts, -0.22, 0.18) if cuts else 1.0
    drawn = jax.random.normal(stream_key, dims, jnp.float32) * deviation * level
    return jnp.minimum(jnp.maximum(drawn, -reach), reach).astype(held_as)


def setup_inputs(seed: int = 0) -> dict:
    splits = jax.random.split(jax.random.key(seed), 5)
    traces = normal_values(splits[0], (NI, NX, NT), 1.0, 6.0, ((0, 4), (1, 2), (2, 4)), jnp.float32)
    live = place_ends((jax.random.randint(splits[1], (NI, NX), 0, 2) < 1).astype(jnp.int32), jax.random.fold_in(splits[1], 1), 0, 1)
    counts = draw_counts(jax.random.fold_in(splits[4], 71), 0)
    levels = draw_levels(jax.random.fold_in(splits[4], 71), 0)
    return {"traces": traces, "live": live, "counts": counts, "levels": levels}


highest = lax.Precision.HIGHEST

def cosine_table(order):
    rows = jnp.arange(order, dtype=jnp.float32)[:, None]
    columns = jnp.arange(order, dtype=jnp.float32)[None, :]
    table = jnp.sqrt(2.0 / order) * jnp.cos(jnp.pi * (2.0 * columns + 1.0) * rows / (2.0 * order))
    scaling = jnp.where(rows == 0, jnp.sqrt(0.5), 1.0)
    return (table * scaling).astype(jnp.float32)

def taper_table(order):
    centres = jnp.arange(order, dtype=jnp.float32) + 0.5
    return jnp.sin(jnp.pi * centres / order) ** 2

def forward(volume, space_table, time_table):
    result = jnp.einsum('ak,ijk->ija', time_table, volume, precision=highest)
    result = jnp.einsum('bj,ija->iba', space_table, result, precision=highest)
    return jnp.einsum('ci,iba->cba', space_table, result, precision=highest)

def inverse(volume, space_table, time_table):
    result = jnp.einsum('ci,cba->iba', space_table, volume, precision=highest)
    result = jnp.einsum('bj,iba->ija', space_table, result, precision=highest)
    return jnp.einsum('ak,ija->ijk', time_table, result, precision=highest)

def reconstruct(window, window_mask, iterations, thresholds, space_table, time_table, taper):
    keep_part = (1.0 - window_mask)[:, :, None]

    def iterate(step_index, estimate):
        coefficients = forward(estimate, space_table, time_table)
        threshold = thresholds[step_index]
        shrunk = coefficients - jnp.clip(coefficients, -threshold, threshold)
        return window + keep_part * inverse(shrunk, space_table, time_table)
    estimate = lax.fori_loop(0, iterations, iterate, window)
    return estimate * taper

def reference(traces, live, counts, levels):
    live_mask = live.astype(jnp.float32)
    observed = jnp.pad(traces * live_mask[:, :, None], ((HALO, HALO), (HALO, HALO), (HALO_T, HALO_T)))
    live_pad = jnp.pad(live_mask, HALO)
    thresholds = levels.astype(jnp.float32) * 0.001
    space_table = cosine_table(WIN)
    time_table = cosine_table(WIN_T)
    space_taper = taper_table(WIN)
    taper = space_taper[:, None, None] * space_taper[None, :, None] * taper_table(WIN_T)[None, None, :]
    windows_time = WPD * N_TA
    flat_counts = counts.reshape(-1)

    def add_window(totals, window_index):
        first = window_index // (N_XL * windows_time)
        second = window_index // windows_time % N_XL
        third = window_index % windows_time
        start_i = (first * CORE).astype(jnp.int32)
        start_x = (second * CORE).astype(jnp.int32)
        start_t = (third * CORE_T).astype(jnp.int32)
        window = lax.dynamic_slice(observed, (start_i, start_x, start_t), (WIN, WIN, WIN_T))
        window_mask = lax.dynamic_slice(live_pad, (start_i, start_x), (WIN, WIN))
        result = reconstruct(window, window_mask, flat_counts[window_index], thresholds, space_table, time_table, taper)
        current = lax.dynamic_slice(totals, (start_i, start_x, start_t), (WIN, WIN, WIN_T))
        return (lax.dynamic_update_slice(totals, current + result, (start_i, start_x, start_t)), None)
    totals, _ = lax.scan(add_window, jnp.zeros(observed.shape, jnp.float32), jnp.arange(N_IL * N_XL * windows_time, dtype=jnp.int32))
    return totals[HALO:HALO + NI, HALO:HALO + NX, HALO_T:HALO_T + NT]
```

```python
import functools

import jax
import jax.numpy as jnp
import numpy as np
from jax import lax
from jax.experimental import pallas as pl
from jax.experimental.pallas import tpu as pltpu
from jax.sharding import PartitionSpec as P

WIN = 64
WIN_T = 128
WPD = 2
HALO = 16
HALO_T = 32
CORE_T = 64
DEAD = 1e30
PITCH = 72
GROUP = 16


def padded(block, sides, width):
    for axis, dim in sides:
        count = lax.axis_size(axis)
        forward = [(i, i + 1) for i in range(count - 1)]
        backward = [(target, source) for source, target in forward]
        low = lax.ppermute(
            lax.slice_in_dim(block, block.shape[dim] - width, None, axis=dim), axis, forward
        )
        high = lax.ppermute(lax.slice_in_dim(block, 0, width, axis=dim), axis, backward)
        block = jnp.concatenate([low, block, high], axis=dim)
    return block


def from_partner(value, axis, stride):
    return lax.ppermute(value, axis, [(i, i ^ 1 << stride) for i in range(lax.axis_size(axis))])


def cosine_table(order):
    rows = np.arange(order, dtype=np.float64)[:, None]
    columns = np.arange(order, dtype=np.float64)[None, :]
    table = np.sqrt(2.0 / order) * np.cos(np.pi * (2.0 * columns + 1.0) * rows / (2.0 * order))
    return table * np.where(rows == 0, np.sqrt(0.5), 1.0)


def taper_table(order):
    centres = np.arange(order, dtype=np.float64) + 0.5
    return np.sin(np.pi * centres / order) ** 2


def halves(table):
    high = table.astype(jnp.bfloat16)
    low = (table - high.astype(np.float64)).astype(jnp.bfloat16)
    return high, low


def tables():
    out = []
    space = cosine_table(WIN)
    for table in (space, space.T):
        high, low = halves(table)
        out.append(np.concatenate([high, high, low], axis=1))
    time = cosine_table(WIN_T)
    for table in (time.T, time):
        high, low = halves(table)
        row = np.concatenate([high, low], axis=1)
        out.append(np.concatenate([row, row], axis=0))
    plane = taper_table(WIN)[:, None] * taper_table(WIN_T)[None, :]
    lines = np.repeat(taper_table(WIN)[:, None], WIN_T, axis=1)
    return [jnp.asarray(t) for t in out] + [
        jnp.asarray(plane, jnp.float32),
        jnp.asarray(lines, jnp.float32),
    ]


def split(value):
    high = value.astype(jnp.bfloat16)
    low = (value - high.astype(jnp.float32)).astype(jnp.bfloat16)
    return high, low


def along_rows(table, slices):
    out = []
    for n in range(0, len(slices), 2):
        high, low = split(jnp.concatenate([slices[n], slices[n + 1]], axis=1))
        both = jnp.dot(
            table, jnp.concatenate([high, low, high], axis=0), preferred_element_type=jnp.float32
        )
        out += [both[:, :WIN_T], both[:, WIN_T:]]
    return out


def along_lanes(table, slices):
    high, low = split(jnp.concatenate(slices, axis=0))
    both = jnp.dot(
        jnp.concatenate([high, low], axis=1), table, preferred_element_type=jnp.float32
    )
    total = both[:, :WIN_T] + both[:, WIN_T:]
    return [total[n * WIN : (n + 1) * WIN] for n in range(len(slices))]


def shrink_kernel(
    counts, levels, window, space_f, space_b, time_f, time_b, plane, lines, out, held
):
    slot = pl.program_id(0)
    last = counts[slot] - 1

    def forward(group, estimates):
        done = along_rows(space_f[...], along_lanes(time_f[...], estimates))
        for n in range(GROUP):
            start = pl.multiple_of((group * GROUP + n) * PITCH, 8)
            held[pl.ds(start, WIN), :] = done[n]

    def recorded(group, n):
        start = pl.multiple_of((group * GROUP + n) * WIN, 8)
        return window[0, pl.ds(start, WIN), :]

    def backward(group):
        slices = []
        for n in range(GROUP):
            start = pl.multiple_of((group * GROUP + n) * PITCH, 8)
            slices.append(held[pl.ds(start, WIN), :])
        guesses = along_lanes(time_b[...], along_rows(space_b[...], slices))
        estimates = []
        for n in range(GROUP):
            known = recorded(group, n)
            estimates.append(jnp.where(known == DEAD, guesses[n], known))
        return estimates

    @pl.loop(0, WIN // GROUP)
    def _(group):
        estimates = []
        for n in range(GROUP):
            known = recorded(group, n)
            estimates.append(jnp.where(known == DEAD, 0.0, known))
        forward(group, estimates)

    def shrink(step):
        threshold = levels[step].astype(jnp.float32) * 0.001

        @pl.loop(0, WIN // GROUP)
        def _(group):
            first = group * GROUP
            places = [pl.ds(first + n, WIN, stride=PITCH) for n in range(GROUP)]
            values = along_rows(space_f[...], [held[p, :] for p in places])
            values = [v - jnp.clip(v, -threshold, threshold) for v in values]
            values = along_rows(space_b[...], values)
            for n in range(GROUP):
                held[places[n], :] = values[n]

    @pl.loop(0, last)
    def _(step):
        shrink(step)

        @pl.loop(0, WIN // GROUP)
        def _(group):
            forward(group, backward(group))

    shrink(last)

    @pl.loop(0, WIN // GROUP)
    def _(group):
        estimates = backward(group)
        for n in range(GROUP):
            line = group * GROUP + n
            start = pl.multiple_of(line * WIN, 8)
            weight = lines[pl.ds(line, 1), :]
            out[0, pl.ds(start, WIN), :] = estimates[n] * (plane[...] * weight)


def reconstruct(windows, counts, levels):
    slots = windows.shape[0]
    fixed = tables()
    whole = [pl.BlockSpec(memory_space=pltpu.VMEM)] * len(fixed)
    block = pl.BlockSpec((1, WIN * WIN, WIN_T), lambda slot, counts, levels: (slot, 0, 0))
    return pl.pallas_call(
        shrink_kernel,
        grid_spec=pltpu.PrefetchScalarGridSpec(
            num_scalar_prefetch=2,
            grid=(slots,),
            in_specs=[block] + whole,
            out_specs=block,
            scratch_shapes=[pltpu.VMEM((WIN * PITCH, WIN_T), jnp.float32)],
        ),
        out_shape=jax.ShapeDtypeStruct(windows.shape, jnp.float32),
        compiler_params=pltpu.CompilerParams(vmem_limit_bytes=40 * 2**20),
        name="shrink",
    )(counts, levels, windows, *fixed)


def fold_margins(block, dim, width):
    extent = block.shape[dim]
    inner = extent - 4 * width
    middle = lax.slice_in_dim(block, 2 * width, 2 * width + inner, axis=dim)
    lower_rim = lax.slice_in_dim(block, 0, width, axis=dim)
    upper_rim = lax.slice_in_dim(block, extent - width, extent, axis=dim)
    lower_pad = [(0, inner - width) if axis_number == dim else (0, 0) for axis_number in range(3)]
    upper_pad = [(inner - width, 0) if axis_number == dim else (0, 0) for axis_number in range(3)]
    return middle + jnp.pad(lower_rim, lower_pad) + jnp.pad(upper_rim, upper_pad)


def shards(traces, live, counts, levels):
    live_mask = live.astype(jnp.float32)
    timed = padded(traces * live_mask[:, :, None], (("ta", 2),), HALO_T)
    observed = padded(timed, (("il", 0), ("xl", 1)), HALO)
    live_pad = padded(live.astype(jnp.bfloat16), (("il", 0), ("xl", 1)), HALO).astype(jnp.float32)
    observed = jnp.where(live_pad[:, :, None] == 0.0, DEAD, observed)
    position = lax.axis_index("xl")
    line_counts = counts[0]
    own = lax.dynamic_index_in_dim(line_counts, position, 0, keepdims=False)
    other = lax.dynamic_index_in_dim(line_counts, jnp.bitwise_xor(position, 1), 0, keepdims=False)
    before = jnp.maximum(own[0] + own[1], other[0] + other[1])
    after = jnp.maximum(own[0] + other[1], other[0] + own[1])
    trading = after < before
    windows = [
        observed[:, :, slot * CORE_T : slot * CORE_T + WIN_T].reshape(WIN * WIN, WIN_T)
        for slot in range(WPD)
    ]
    arrived = from_partner(windows[1], "xl", 0)
    windows[1] = jnp.where(trading, arrived, windows[1])
    work = jnp.stack([own[0], jnp.where(trading, other[1], own[1])])
    done = reconstruct(jnp.stack(windows), work, levels)
    results = [done[0], jnp.where(trading, from_partner(done[1], "xl", 0), done[1])]
    results = [r.reshape(WIN, WIN, WIN_T) for r in results]
    accumulated = jnp.pad(results[0], ((0, 0), (0, 0), (0, CORE_T)))
    accumulated = accumulated + jnp.pad(results[1], ((0, 0), (0, 0), (CORE_T, 0)))
    spread = padded(accumulated, (("il", 0), ("xl", 1)), HALO)
    spread = fold_margins(spread, 0, HALO)
    spread = fold_margins(spread, 1, HALO)
    spread = padded(spread, (("ta", 2),), HALO_T)
    return fold_margins(spread, 2, HALO_T)


def solution(mesh):
    placed = (P("il", "xl", "ta"), P("il", "xl"), P("il", None, "ta"), P())
    return jax.shard_map(
        shards, mesh=mesh, in_specs=placed, out_specs=P("il", "xl", "ta"), check_vma=False
    )
```

```python
import functools

import jax
import jax.numpy as jnp
import numpy as np
from jax import lax
from jax.experimental import pallas as pl
from jax.experimental.pallas import tpu as pltpu
from jax.sharding import PartitionSpec as P

WIN = 64
WIN_T = 128
WPD = 2
HALO = 16
HALO_T = 32
DEAD = 1e30
PITCH = 72
GROUP = 16


def cosine_table(order):
    rows = np.arange(order, dtype=np.float64)[:, None]
    columns = np.arange(order, dtype=np.float64)[None, :]
    table = np.sqrt(2.0 / order) * np.cos(np.pi * (2.0 * columns + 1.0) * rows / (2.0 * order))
    return table * np.where(rows == 0, np.sqrt(0.5), 1.0)


def taper_table(order):
    centres = np.arange(order, dtype=np.float64) + 0.5
    return np.sin(np.pi * centres / order) ** 2


def halves(table):
    high = table.astype(jnp.bfloat16)
    low = (table - high.astype(np.float64)).astype(jnp.bfloat16)
    return high, low


def tables():
    out = []
    space = cosine_table(WIN)
    for table in (space, space.T):
        high, low = halves(table)
        out.append(np.concatenate([high, high, low], axis=1))
    time = cosine_table(WIN_T)
    for table in (time.T, time):
        high, low = halves(table)
        row = np.concatenate([high, low], axis=1)
        out.append(np.concatenate([row, row], axis=0))
    plane = taper_table(WIN)[:, None] * taper_table(WIN_T)[None, :]
    lines = np.repeat(taper_table(WIN)[:, None], WIN_T, axis=1)
    return [jnp.asarray(t) for t in out] + [
        jnp.asarray(plane, jnp.float32),
        jnp.asarray(lines, jnp.float32),
    ]


def split(value):
    high = value.astype(jnp.bfloat16)
    low = (value - high.astype(jnp.float32)).astype(jnp.bfloat16)
    return high, low


def along_rows(table, slices):
    out = []
    for n in range(0, len(slices), 2):
        high, low = split(jnp.concatenate([slices[n], slices[n + 1]], axis=1))
        both = jnp.dot(
            table, jnp.concatenate([high, low, high], axis=0), preferred_element_type=jnp.float32
        )
        out += [both[:, :WIN_T], both[:, WIN_T:]]
    return out


def along_lanes(table, slices):
    high, low = split(jnp.concatenate(slices, axis=0))
    both = jnp.dot(
        jnp.concatenate([high, low], axis=1), table, preferred_element_type=jnp.float32
    )
    total = both[:, :WIN_T] + both[:, WIN_T:]
    return [total[n * WIN : (n + 1) * WIN] for n in range(len(slices))]


def shrink_kernel(
    counts, places, levels, window, space_f, space_b, time_f, time_b, plane, lines, out, held
):
    slot = pl.program_id(0)
    last = counts[slot] - 1

    def forward(group, estimates):
        done = along_rows(space_f[...], along_lanes(time_f[...], estimates))
        for n in range(GROUP):
            start = pl.multiple_of((group * GROUP + n) * PITCH, 8)
            held[pl.ds(start, WIN), :] = done[n]

    def recorded(group, n):
        start = pl.multiple_of((group * GROUP + n) * WIN, 8)
        return window[0, pl.ds(start, WIN), :]

    def backward(group):
        slices = []
        for n in range(GROUP):
            start = pl.multiple_of((group * GROUP + n) * PITCH, 8)
            slices.append(held[pl.ds(start, WIN), :])
        guesses = along_lanes(time_b[...], along_rows(space_b[...], slices))
        estimates = []
        for n in range(GROUP):
            known = recorded(group, n)
            estimates.append(jnp.where(known == DEAD, guesses[n], known))
        return estimates

    @pl.loop(0, WIN // GROUP)
    def _(group):
        estimates = []
        for n in range(GROUP):
            known = recorded(group, n)
            estimates.append(jnp.where(known == DEAD, 0.0, known))
        forward(group, estimates)

    def shrink(step):
        threshold = levels[step].astype(jnp.float32) * 0.001

        @pl.loop(0, WIN // GROUP)
        def _(group):
            first = group * GROUP
            rows = [pl.ds(first + n, WIN, stride=PITCH) for n in range(GROUP)]
            values = along_rows(space_f[...], [held[r, :] for r in rows])
            values = [v - jnp.clip(v, -threshold, threshold) for v in values]
            values = along_rows(space_b[...], values)
            for n in range(GROUP):
                held[rows[n], :] = values[n]

    @pl.loop(0, last)
    def _(step):
        shrink(step)

        @pl.loop(0, WIN // GROUP)
        def _(group):
            forward(group, backward(group))

    shrink(last)

    @pl.loop(0, WIN // GROUP)
    def _(group):
        estimates = backward(group)
        for n in range(GROUP):
            line = group * GROUP + n
            start = pl.multiple_of(line * WIN, 8)
            weight = lines[pl.ds(line, 1), :]
            out[0, pl.ds(start, WIN), :] = estimates[n] * (plane[...] * weight)


def reconstruct(windows, counts, places, levels):
    slots = counts.shape[0]
    fixed = tables()
    whole = [pl.BlockSpec(memory_space=pltpu.VMEM)] * len(fixed)
    shape = (1, WIN * WIN, WIN_T)
    block = pl.BlockSpec(shape, lambda slot, counts, places, levels: (places[slot], 0, 0))
    result = pl.BlockSpec(shape, lambda slot, counts, places, levels: (slot, 0, 0))
    return pl.pallas_call(
        shrink_kernel,
        grid_spec=pltpu.PrefetchScalarGridSpec(
            num_scalar_prefetch=3,
            grid=(slots,),
            in_specs=[block] + whole,
            out_specs=result,
            scratch_shapes=[pltpu.VMEM((WIN * PITCH, WIN_T), jnp.float32)],
        ),
        out_shape=jax.ShapeDtypeStruct((slots,) + windows.shape[1:], jnp.float32),
        compiler_params=pltpu.CompilerParams(vmem_limit_bytes=40 * 2**20),
        name="shrink",
    )(counts, places, levels, windows, *fixed)


class Links:
    def __init__(self, sizes, send_sems, recv_sems):
        self.sizes, self.send_sems, self.recv_sems = sizes, send_sems, recv_sems
        self.me = {axis: lax.axis_index(axis) for axis in sizes}
        self.used = 0

    def has(self, axis, step):
        if step > 0:
            return self.me[axis] < self.sizes[axis] - 1
        return self.me[axis] > 0

    def barrier(self):
        barrier = pltpu.get_barrier_semaphore()
        total = 0
        for axis in self.sizes:
            for step in (-1, 1):
                there = self.has(axis, step)
                total = total + there.astype(jnp.int32)

                @pl.when(there)
                def _():
                    pl.semaphore_signal(
                        barrier,
                        inc=1,
                        device_id={axis: self.me[axis] + step},
                        device_id_type=pl.DeviceIdType.MESH,
                    )

        pl.semaphore_wait(barrier, total)

    def copy(self, source, target, axis, index):
        number = self.used
        self.used += 1
        return pltpu.make_async_remote_copy(
            src_ref=source,
            dst_ref=target,
            send_sem=self.send_sems.at[number],
            recv_sem=self.recv_sems.at[number],
            device_id={axis: index},
            device_id_type=pl.DeviceIdType.MESH,
        )

    def send(self, source, target, axis, step):
        copy = self.copy(source, target, axis, self.me[axis] + step)

        @pl.when(self.has(axis, step))
        def _():
            copy.start()

        return copy, axis, step

    def arrive(self, sent, otherwise=None):
        copy, axis, step = sent
        there = self.has(axis, -step)

        @pl.when(there)
        def _():
            copy.wait_recv()

        if otherwise is not None:

            @pl.when(jnp.logical_not(there))
            def _():
                otherwise()

    def finish(self, sents):
        for copy, axis, step in sents:

            @pl.when(self.has(axis, step))
            def _():
                copy.wait_send()

    def partner(self, source, target):
        me = self.me["xl"]
        return self.copy(source, target, "xl", me + 1 - 2 * lax.rem(me, 2))


QUARTERS = WIN_T // HALO_T
UNIT = HALO // QUARTERS


def lane_numbers(shape):
    return lax.broadcasted_iota(jnp.int32, shape, len(shape) - 1)


def turned(value, shift):
    shift = shift % WIN_T
    return pltpu.roll(value, shift, value.ndim - 1) if shift else value


def pieces(parts):
    for h in range(parts):
        for q in range(QUARTERS):
            start = h * HALO + q * UNIT
            yield h, q, pl.ds(start, UNIT), pl.ds(h * UNIT, UNIT)


def in_quarter(lanes, q):
    return (lanes >= q * HALO_T) & (lanes < (q + 1) * HALO_T)


def gather_kernel(sizes, mine, out, raw, early, late, to_next, to_prev, send_sems, recv_sems):
    links = Links(sizes, send_sems, recv_sems)
    links.barrier()
    core_i, core_x, _ = mine.shape
    inner_x = pl.ds(HALO, core_x)
    low_i, high_i = pl.ds(0, HALO), pl.ds(HALO + core_i, HALO)
    sent = []

    def send(*args):
        sent.append(links.send(*args))
        return sent[-1]

    raw_up = send(mine.at[pl.ds(core_i - HALO, HALO)], raw.at[low_i, inner_x], "il", 1)
    raw_down = send(mine.at[pl.ds(0, HALO)], raw.at[high_i, inner_x], "il", -1)

    for h, q, span, row in pieces(core_i // HALO):
        block = mine[span]
        lanes = lane_numbers(block.shape)
        chosen = in_quarter(lanes, q)
        first = turned(block, q * HALO_T)
        final = turned(block, q * HALO_T - (WIN_T - HALO_T))
        to_prev[row] = first if q == 0 else jnp.where(chosen, first, to_prev[row])
        to_next[row] = final if q == 0 else jnp.where(chosen, final, to_next[row])

    inner_p = pl.ds(UNIT, core_i // QUARTERS)
    early_in = send(to_next, early.at[inner_p, inner_x], "ta", 1)
    late_in = send(to_prev, late.at[inner_p, inner_x], "ta", -1)
    raw[pl.ds(HALO, core_i), inner_x] = mine[...]

    def blank(target, source):
        def fill():
            target[inner_p, inner_x] = jnp.where(source[...] == DEAD, DEAD, 0.0)

        return fill

    low_p, high_p = pl.ds(0, UNIT), pl.ds(UNIT + core_i // QUARTERS, UNIT)
    from_p = pl.ds(core_i // QUARTERS, UNIT)
    waits = [(raw_up, raw, low_i), (raw_down, raw, high_i)]
    for arrival, buffer, source in ((early_in, early, to_next), (late_in, late, to_prev)):
        links.arrive(arrival, blank(buffer, source))
        up = send(buffer.at[from_p, inner_x], buffer.at[low_p, inner_x], "il", 1)
        down = send(buffer.at[pl.ds(UNIT, UNIT), inner_x], buffer.at[high_p, inner_x], "il", -1)
        waits += [(up, buffer, low_p), (down, buffer, high_p)]

    def missing(target, first, second):
        def fill():
            shape = target.at[first, second].shape
            target[first, second] = jnp.full(shape, DEAD, jnp.float32)

        return fill

    for arrival, buffer, place in waits:
        links.arrive(arrival, missing(buffer, place, inner_x))

    waits = []
    low_x, high_x = pl.ds(0, HALO), pl.ds(HALO + core_x, HALO)
    for buffer in (raw, early, late):
        whole = pl.ds(0, buffer.shape[0])
        up = send(buffer.at[whole, pl.ds(core_x, HALO)], buffer.at[whole, low_x], "xl", 1)
        down = send(buffer.at[whole, pl.ds(HALO, HALO)], buffer.at[whole, high_x], "xl", -1)
        waits += [(up, buffer, low_x), (down, buffer, high_x)]
    for arrival, buffer, place in waits:
        links.arrive(arrival, missing(buffer, pl.ds(0, buffer.shape[0]), place))

    for h, q, span, row in pieces(WIN // HALO):
        block = raw[span]
        lanes = lane_numbers(block.shape)
        added = turned(late[row], WIN_T - HALO_T - q * HALO_T)
        out[1, span] = jnp.where(lanes < WIN_T - HALO_T, turned(block, -HALO_T), added)
    trade = links.partner(out.at[1], out.at[2])
    trade.start()
    for h, q, span, row in pieces(WIN // HALO):
        block = raw[span]
        lanes = lane_numbers(block.shape)
        added = turned(early[row], -q * HALO_T)
        out[0, span] = jnp.where(lanes < HALO_T, added, turned(block, HALO_T))
    trade.wait()
    links.finish(sent)


def gather_windows(coded, sizes):
    packed = (WIN // QUARTERS, WIN, WIN_T)
    small = (coded.shape[0] // QUARTERS, coded.shape[1], WIN_T)
    scratch = [(WIN, WIN, WIN_T), packed, packed, small, small]
    return pl.pallas_call(
        functools.partial(gather_kernel, sizes),
        out_shape=jax.ShapeDtypeStruct((3, WIN, WIN, WIN_T), jnp.float32),
        in_specs=[pl.BlockSpec(memory_space=pltpu.VMEM)],
        out_specs=pl.BlockSpec(memory_space=pltpu.VMEM),
        scratch_shapes=[pltpu.VMEM(shape, jnp.float32) for shape in scratch]
        + [pltpu.SemaphoreType.DMA((15,)), pltpu.SemaphoreType.DMA((15,))],
        compiler_params=pltpu.CompilerParams(
            collective_id=0, has_side_effects=True, vmem_limit_bytes=40 * 2**20
        ),
        name="gather_windows",
    )(coded)


def scatter_kernel(
    sizes,
    flag,
    done,
    out,
    foreign,
    raw,
    early,
    late,
    side_raw,
    side_early,
    side_late,
    edge_raw,
    edge_early,
    edge_late,
    from_time,
    send_sems,
    recv_sems,
):
    links = Links(sizes, send_sems, recv_sems)
    links.barrier()
    core_i, core_x, _ = out.shape
    inner_x = pl.ds(HALO, core_x)
    sent = []

    def send(*args):
        sent.append(links.send(*args))
        return sent[-1]

    trade = links.partner(done.at[1], foreign)
    trade.start()
    for h, q, span, row in pieces(WIN // HALO):
        block = done[0, span]
        lanes = lane_numbers(block.shape)
        raw[span] = jnp.where(lanes < WIN_T - HALO_T, turned(block, -HALO_T), 0.0)
        first = turned(block, q * HALO_T)
        early[row] = first if q == 0 else jnp.where(in_quarter(lanes, q), first, early[row])
    trade.wait()
    for h, q, span, row in pieces(WIN // HALO):
        block = jnp.where(flag[...][None, :1, :] > 0.5, foreign[span], done[1, span])
        lanes = lane_numbers(block.shape)
        raw[span] = raw[span] + jnp.where(lanes >= HALO_T, turned(block, HALO_T), 0.0)
        final = turned(block, q * HALO_T - (WIN_T - HALO_T))
        late[row] = final if q == 0 else jnp.where(in_quarter(lanes, q), final, late[row])

    def add(target, first, second, source):
        there = target[first, second]
        target[first, second] = there + source[...]

    waits = []
    for buffer, side in ((raw, side_raw), (early, side_early), (late, side_late)):
        whole = pl.ds(0, buffer.shape[0])
        down = send(buffer.at[whole, pl.ds(0, HALO)], side.at[0], "xl", -1)
        up = send(buffer.at[whole, pl.ds(HALO + core_x, HALO)], side.at[1], "xl", 1)
        waits += [
            (down, buffer, whole, pl.ds(core_x, HALO), side.at[0]),
            (up, buffer, whole, pl.ds(HALO, HALO), side.at[1]),
        ]

    def gathered(waits):
        for arrival, buffer, first, second, source in waits:
            links.arrive(arrival)
            _, axis, step = arrival

            @pl.when(links.has(axis, -step))
            def _():
                add(buffer, first, second, source)

    gathered(waits)

    waits = []
    for buffer, edge, width in (
        (early, edge_early, UNIT),
        (late, edge_late, UNIT),
        (raw, edge_raw, HALO),
    ):
        total = buffer.shape[0]
        inner = total - 2 * width
        down = send(buffer.at[pl.ds(0, width), inner_x], edge.at[0], "il", -1)
        up = send(buffer.at[pl.ds(total - width, width), inner_x], edge.at[1], "il", 1)
        waits += [
            (down, buffer, pl.ds(inner, width), inner_x, edge.at[0]),
            (up, buffer, pl.ds(width, width), inner_x, edge.at[1]),
        ]
    gathered(waits[:4])
    inner_p = pl.ds(UNIT, core_i // QUARTERS)
    back = send(early.at[inner_p, inner_x], from_time.at[0], "ta", -1)
    ahead = send(late.at[inner_p, inner_x], from_time.at[1], "ta", 1)
    gathered(waits[4:])
    out[...] = raw[pl.ds(HALO, core_i), inner_x]
    for arrival, side, shift in ((back, 0, WIN_T - HALO_T), (ahead, 1, 0)):
        links.arrive(arrival)
        _, axis, step = arrival

        @pl.when(links.has(axis, -step))
        def _():
            for h, q, span, row in pieces(core_i // HALO):
                block = turned(from_time[side, row], shift - q * HALO_T)
                lanes = lane_numbers(block.shape)
                kept = in_quarter(lanes, shift // HALO_T)
                out[span] = out[span] + jnp.where(kept, block, 0.0)

    links.finish(sent)


def scatter_windows(flag, done, shape, sizes):
    core_i, core_x, _ = shape
    packed = (WIN // QUARTERS, WIN, WIN_T)
    small = (WIN // QUARTERS, HALO, WIN_T)
    scratch = [
        (WIN, WIN, WIN_T),
        (WIN, WIN, WIN_T),
        packed,
        packed,
        (2, WIN, HALO, WIN_T),
        (2,) + small,
        (2,) + small,
        (2, HALO, core_x, WIN_T),
        (2, UNIT, core_x, WIN_T),
        (2, UNIT, core_x, WIN_T),
        (2, core_i // QUARTERS, core_x, WIN_T),
    ]
    return pl.pallas_call(
        functools.partial(scatter_kernel, sizes),
        out_shape=jax.ShapeDtypeStruct(shape, jnp.float32),
        in_specs=[pl.BlockSpec(memory_space=pltpu.VMEM)] * 2,
        out_specs=pl.BlockSpec(memory_space=pltpu.VMEM),
        scratch_shapes=[pltpu.VMEM(shape, jnp.float32) for shape in scratch]
        + [pltpu.SemaphoreType.DMA((15,)), pltpu.SemaphoreType.DMA((15,))],
        compiler_params=pltpu.CompilerParams(
            collective_id=1, has_side_effects=True, vmem_limit_bytes=40 * 2**20
        ),
        name="scatter_windows",
    )(flag, done)


def shards(sizes, traces, live, counts, levels):
    coded = jnp.where(live[:, :, None] == 0, DEAD, traces)
    windows = gather_windows(coded, sizes).reshape(3, WIN * WIN, WIN_T)
    position = lax.axis_index("xl")
    line_counts = counts[0]
    own = lax.dynamic_index_in_dim(line_counts, position, 0, keepdims=False)
    other = lax.dynamic_index_in_dim(line_counts, jnp.bitwise_xor(position, 1), 0, keepdims=False)
    before = jnp.maximum(own[0] + own[1], other[0] + other[1])
    after = jnp.maximum(own[0] + other[1], other[0] + own[1])
    trading = after < before
    work = jnp.stack([own[0], jnp.where(trading, other[1], own[1])])
    places = jnp.stack([jnp.int32(0), jnp.where(trading, 2, 1)])
    done = reconstruct(windows, work, places, levels)
    flag = jnp.full((8, WIN_T), trading.astype(jnp.float32))
    return scatter_windows(flag, done.reshape(WPD, WIN, WIN, WIN_T), traces.shape, sizes)


def solution(mesh):
    placed = (P("il", "xl", "ta"), P("il", "xl"), P("il", None, "ta"), P())
    sizes = {axis: mesh.shape[axis] for axis in ("il", "xl", "ta")}
    return jax.shard_map(
        functools.partial(shards, sizes),
        mesh=mesh,
        in_specs=placed,
        out_specs=P("il", "xl", "ta"),
        check_vma=False,
    )
```

```python
import functools

import jax
import jax.numpy as jnp
import numpy as np
from jax import lax
from jax.experimental import pallas as pl
from jax.experimental.pallas import tpu as pltpu
from jax.sharding import PartitionSpec as P

WIN = 64
WIN_T = 128
WPD = 2
HALO = 16
HALO_T = 32
DEAD = 1e30
PITCH = 72
GROUP = 16


def cosine_table(order):
    rows = np.arange(order, dtype=np.float64)[:, None]
    columns = np.arange(order, dtype=np.float64)[None, :]
    table = np.sqrt(2.0 / order) * np.cos(np.pi * (2.0 * columns + 1.0) * rows / (2.0 * order))
    return table * np.where(rows == 0, np.sqrt(0.5), 1.0)


def taper_table(order):
    centres = np.arange(order, dtype=np.float64) + 0.5
    return np.sin(np.pi * centres / order) ** 2


def halves(table):
    high = table.astype(jnp.bfloat16)
    low = (table - high.astype(np.float64)).astype(jnp.bfloat16)
    return high, low


def tables():
    out = []
    space = cosine_table(WIN)
    for table in (space, space.T):
        high, low = halves(table)
        upper = np.concatenate([high, high], axis=1)
        out.append(np.concatenate([upper, np.concatenate([low, 0 * low], axis=1)], axis=0))
    time = cosine_table(WIN_T)
    for table in (time.T, time):
        high, low = halves(table)
        row = np.concatenate([high, low], axis=1)
        out.append(np.concatenate([row, row], axis=0))
    plane = taper_table(WIN)[:, None] * taper_table(WIN_T)[None, :]
    lines = np.repeat(taper_table(WIN)[:, None], WIN_T, axis=1)
    return [jnp.asarray(t) for t in out] + [
        jnp.asarray(plane, jnp.float32),
        jnp.asarray(lines, jnp.float32),
    ]


def split(value):
    high = value.astype(jnp.bfloat16)
    low = (value - high.astype(jnp.float32)).astype(jnp.bfloat16)
    return high, low


def along_rows(table, slices):
    out = []
    for n in range(0, len(slices), 2):
        high, low = split(jnp.concatenate([slices[n], slices[n + 1]], axis=1))
        both = jnp.dot(
            table, jnp.concatenate([high, low], axis=0), preferred_element_type=jnp.float32
        )
        both = both[:WIN] + both[WIN:]
        out += [both[:, :WIN_T], both[:, WIN_T:]]
    return out


def along_lanes(table, slices):
    high, low = split(jnp.concatenate(slices, axis=0))
    both = jnp.dot(
        jnp.concatenate([high, low], axis=1), table, preferred_element_type=jnp.float32
    )
    total = both[:, :WIN_T] + both[:, WIN_T:]
    return [total[n * WIN : (n + 1) * WIN] for n in range(len(slices))]


def shrink_kernel(
    counts,
    levels,
    windows,
    space_f,
    space_b,
    time_f,
    time_b,
    plane,
    lines,
    out,
    flag,
    held,
    window,
    ready,
    in_sems,
    out_sems,
):
    me = lax.axis_index("xl")
    other = me + 1 - 2 * lax.rem(me, 2)
    own_first, own_final = counts[WPD * me], counts[WPD * me + 1]
    other_first, other_final = counts[WPD * other], counts[WPD * other + 1]
    before = jnp.maximum(own_first + own_final, other_first + other_final)
    after = jnp.maximum(own_first + other_final, other_first + own_final)
    trading = after < before
    flag[...] = jnp.full(flag.shape, jnp.where(trading, 1.0, 0.0), jnp.float32)
    second = jnp.where(trading, 2, 1)
    pltpu.make_async_copy(windows.at[0], window.at[0], in_sems.at[0]).start()
    pltpu.make_async_copy(windows.at[second], window.at[1], in_sems.at[1]).start()

    @pl.loop(0, WPD)
    def _(slot):
        pltpu.make_async_copy(windows.at[slot], window.at[slot], in_sems.at[slot]).wait()
        final = jnp.where(trading, other_final, own_final)
        count = jnp.where(slot == 0, own_first, final)
        tables = (space_f, space_b, time_f, time_b, plane, lines)
        shrink_window(count, levels, window.at[slot], *tables, ready.at[slot], held)
        pltpu.make_async_copy(ready.at[slot], out.at[slot], out_sems.at[slot]).start()

    for slot in range(WPD):
        pltpu.make_async_copy(ready.at[slot], out.at[slot], out_sems.at[slot]).wait()


def shrink_window(
    count, levels, window, space_f, space_b, time_f, time_b, plane, lines, out, held
):
    last = count - 1

    def forward(group, estimates):
        done = along_rows(space_f[...], along_lanes(time_f[...], estimates))
        for n in range(GROUP):
            start = pl.multiple_of((group * GROUP + n) * PITCH, 8)
            held[pl.ds(start, WIN), :] = done[n]

    def recorded(group, n):
        start = pl.multiple_of((group * GROUP + n) * WIN, 8)
        return window[pl.ds(start, WIN), :]

    def backward(group):
        slices = []
        for n in range(GROUP):
            start = pl.multiple_of((group * GROUP + n) * PITCH, 8)
            slices.append(held[pl.ds(start, WIN), :])
        guesses = along_lanes(time_b[...], along_rows(space_b[...], slices))
        estimates = []
        for n in range(GROUP):
            known = recorded(group, n)
            estimates.append(jnp.where(known == DEAD, guesses[n], known))
        return estimates

    @pl.loop(0, WIN // GROUP)
    def _(group):
        estimates = []
        for n in range(GROUP):
            known = recorded(group, n)
            estimates.append(jnp.where(known == DEAD, 0.0, known))
        forward(group, estimates)

    def shrink(step):
        threshold = levels[step].astype(jnp.float32) * 0.001

        @pl.loop(0, WIN // GROUP)
        def _(group):
            first = group * GROUP
            rows = [pl.ds(first + n, WIN, stride=PITCH) for n in range(GROUP)]
            values = along_rows(space_f[...], [held[r, :] for r in rows])
            values = [v - jnp.clip(v, -threshold, threshold) for v in values]
            values = along_rows(space_b[...], values)
            for n in range(GROUP):
                held[rows[n], :] = values[n]

    @pl.loop(0, last)
    def _(step):
        shrink(step)

        @pl.loop(0, WIN // GROUP)
        def _(group):
            forward(group, backward(group))

    shrink(last)

    @pl.loop(0, WIN // GROUP)
    def _(group):
        estimates = backward(group)
        for n in range(GROUP):
            line = group * GROUP + n
            start = pl.multiple_of(line * WIN, 8)
            weight = lines[pl.ds(line, 1), :]
            out[pl.ds(start, WIN), :] = estimates[n] * (plane[...] * weight)


def reconstruct(windows, counts, levels):
    fixed = tables()
    shape = (WPD,) + windows.shape[1:]
    vmem = pl.BlockSpec(memory_space=pltpu.VMEM)
    smem = pl.BlockSpec(memory_space=pltpu.SMEM)
    hbm = pl.BlockSpec(memory_space=pl.ANY)
    return pl.pallas_call(
        shrink_kernel,
        in_specs=[smem, smem, hbm] + [vmem] * len(fixed),
        out_specs=[hbm, vmem],
        out_shape=[
            jax.ShapeDtypeStruct(shape, jnp.float32),
            jax.ShapeDtypeStruct((8, WIN_T), jnp.float32),
        ],
        scratch_shapes=[
            pltpu.VMEM((WIN * PITCH, WIN_T), jnp.float32),
            pltpu.VMEM(shape, jnp.float32),
            pltpu.VMEM(shape, jnp.float32),
            pltpu.SemaphoreType.DMA((WPD,)),
            pltpu.SemaphoreType.DMA((WPD,)),
        ],
        compiler_params=pltpu.CompilerParams(vmem_limit_bytes=40 * 2**20),
        name="shrink",
    )(counts, levels, windows, *fixed)


class Links:
    def __init__(self, sizes, send_sems, recv_sems):
        self.sizes, self.send_sems, self.recv_sems = sizes, send_sems, recv_sems
        self.me = {axis: lax.axis_index(axis) for axis in sizes}
        self.used = 0

    def has(self, axis, step):
        if step > 0:
            return self.me[axis] < self.sizes[axis] - 1
        return self.me[axis] > 0

    def barrier(self):
        barrier = pltpu.get_barrier_semaphore()
        total = 0
        for axis in self.sizes:
            for step in (-1, 1):
                there = self.has(axis, step)
                total = total + there.astype(jnp.int32)

                @pl.when(there)
                def _():
                    pl.semaphore_signal(
                        barrier,
                        inc=1,
                        device_id={axis: self.me[axis] + step},
                        device_id_type=pl.DeviceIdType.MESH,
                    )

        pl.semaphore_wait(barrier, total)

    def copy(self, source, target, axis, index):
        number = self.used
        self.used += 1
        return pltpu.make_async_remote_copy(
            src_ref=source,
            dst_ref=target,
            send_sem=self.send_sems.at[number],
            recv_sem=self.recv_sems.at[number],
            device_id={axis: index},
            device_id_type=pl.DeviceIdType.MESH,
        )

    def send(self, source, target, axis, step):
        copy = self.copy(source, target, axis, self.me[axis] + step)

        @pl.when(self.has(axis, step))
        def _():
            copy.start()

        return copy, axis, step

    def arrive(self, sent, otherwise=None):
        copy, axis, step = sent
        there = self.has(axis, -step)

        @pl.when(there)
        def _():
            copy.wait_recv()

        if otherwise is not None:

            @pl.when(jnp.logical_not(there))
            def _():
                otherwise()

    def finish(self, sents):
        for copy, axis, step in sents:

            @pl.when(self.has(axis, step))
            def _():
                copy.wait_send()

    def partner(self, source, target):
        me = self.me["xl"]
        return self.copy(source, target, "xl", me + 1 - 2 * lax.rem(me, 2))


QUARTERS = WIN_T // HALO_T
UNIT = HALO // QUARTERS


def lane_numbers(shape):
    return lax.broadcasted_iota(jnp.int32, shape, len(shape) - 1)


def turned(value, shift):
    shift = shift % WIN_T
    return pltpu.roll(value, shift, value.ndim - 1) if shift else value


def pieces(parts):
    for h in range(parts):
        for q in range(QUARTERS):
            start = h * HALO + q * UNIT
            yield h, q, pl.ds(start, UNIT), pl.ds(h * UNIT, UNIT)


def in_quarter(lanes, q):
    return (lanes >= q * HALO_T) & (lanes < (q + 1) * HALO_T)


def gather_kernel(
    sizes,
    traces,
    live,
    out,
    mine,
    raw,
    early,
    late,
    to_next,
    to_prev,
    ready,
    local_sems,
    send_sems,
    recv_sems,
):
    links = Links(sizes, send_sems, recv_sems)
    core_i, core_x, _ = mine.shape
    square = (core_x, core_x)
    same = lax.broadcasted_iota(jnp.int32, square, 0) == lax.broadcasted_iota(jnp.int32, square, 1)
    spread = [jnp.where(same, live[pl.ds(n, 1), :], 0) for n in range(core_i)]
    spread = jnp.concatenate(spread, axis=0).astype(jnp.float32).astype(jnp.bfloat16)
    ones = jnp.ones((core_x, WIN_T), jnp.bfloat16)
    seen = jnp.dot(spread, ones, preferred_element_type=jnp.float32).reshape(mine.shape)
    mine[...] = jnp.where(seen > 0.5, traces[...], DEAD)
    links.barrier()
    inner_x = pl.ds(HALO, core_x)
    low_i, high_i = pl.ds(0, HALO), pl.ds(HALO + core_i, HALO)
    sent = []

    def send(*args):
        sent.append(links.send(*args))
        return sent[-1]

    raw_up = send(mine.at[pl.ds(core_i - HALO, HALO)], raw.at[low_i, inner_x], "il", 1)
    raw_down = send(mine.at[pl.ds(0, HALO)], raw.at[high_i, inner_x], "il", -1)

    for h, q, span, row in pieces(core_i // HALO):
        block = mine[span]
        lanes = lane_numbers(block.shape)
        chosen = in_quarter(lanes, q)
        first = turned(block, q * HALO_T)
        final = turned(block, q * HALO_T - (WIN_T - HALO_T))
        to_prev[row] = first if q == 0 else jnp.where(chosen, first, to_prev[row])
        to_next[row] = final if q == 0 else jnp.where(chosen, final, to_next[row])

    inner_p = pl.ds(UNIT, core_i // QUARTERS)
    early_in = send(to_next, early.at[inner_p, inner_x], "ta", 1)
    late_in = send(to_prev, late.at[inner_p, inner_x], "ta", -1)
    raw[pl.ds(HALO, core_i), inner_x] = mine[...]

    def blank(target, source):
        def fill():
            target[inner_p, inner_x] = jnp.where(source[...] == DEAD, DEAD, 0.0)

        return fill

    low_p, high_p = pl.ds(0, UNIT), pl.ds(UNIT + core_i // QUARTERS, UNIT)
    from_p = pl.ds(core_i // QUARTERS, UNIT)
    waits = [(raw_up, raw, low_i), (raw_down, raw, high_i)]
    for arrival, buffer, source in ((early_in, early, to_next), (late_in, late, to_prev)):
        links.arrive(arrival, blank(buffer, source))
        up = send(buffer.at[from_p, inner_x], buffer.at[low_p, inner_x], "il", 1)
        down = send(buffer.at[pl.ds(UNIT, UNIT), inner_x], buffer.at[high_p, inner_x], "il", -1)
        waits += [(up, buffer, low_p), (down, buffer, high_p)]

    def missing(target, first, second):
        def fill():
            shape = target.at[first, second].shape
            target[first, second] = jnp.full(shape, DEAD, jnp.float32)

        return fill

    for arrival, buffer, place in waits:
        links.arrive(arrival, missing(buffer, place, inner_x))

    waits = []
    low_x, high_x = pl.ds(0, HALO), pl.ds(HALO + core_x, HALO)
    for buffer in (raw, early, late):
        whole = pl.ds(0, buffer.shape[0])
        up = send(buffer.at[whole, pl.ds(core_x, HALO)], buffer.at[whole, low_x], "xl", 1)
        down = send(buffer.at[whole, pl.ds(HALO, HALO)], buffer.at[whole, high_x], "xl", -1)
        waits += [(up, buffer, low_x), (down, buffer, high_x)]
    for arrival, buffer, place in waits:
        links.arrive(arrival, missing(buffer, pl.ds(0, buffer.shape[0]), place))

    for h, q, span, row in pieces(WIN // HALO):
        block = raw[span]
        lanes = lane_numbers(block.shape)
        added = turned(late[row], WIN_T - HALO_T - q * HALO_T)
        ready[1, span] = jnp.where(lanes < WIN_T - HALO_T, turned(block, -HALO_T), added)
    trade = links.partner(ready.at[1], out.at[2])
    trade.start()
    keep = [pltpu.make_async_copy(ready.at[n], out.at[n], local_sems.at[n]) for n in range(WPD)]
    keep[1].start()
    for h, q, span, row in pieces(WIN // HALO):
        block = raw[span]
        lanes = lane_numbers(block.shape)
        added = turned(early[row], -q * HALO_T)
        ready[0, span] = jnp.where(lanes < HALO_T, added, turned(block, HALO_T))
    keep[0].start()
    keep[0].wait()
    keep[1].wait()
    trade.wait()
    links.finish(sent)


def gather_windows(traces, live, sizes):
    packed = (WIN // QUARTERS, WIN, WIN_T)
    small = (traces.shape[0] // QUARTERS, traces.shape[1], WIN_T)
    scratch = [traces.shape, (WIN, WIN, WIN_T), packed, packed, small, small]
    scratch += [(WPD, WIN, WIN, WIN_T)]
    return pl.pallas_call(
        functools.partial(gather_kernel, sizes),
        out_shape=jax.ShapeDtypeStruct((3, WIN, WIN, WIN_T), jnp.float32),
        in_specs=[pl.BlockSpec(memory_space=pltpu.VMEM)] * 2,
        out_specs=pl.BlockSpec(memory_space=pl.ANY),
        scratch_shapes=[pltpu.VMEM(shape, jnp.float32) for shape in scratch]
        + [pltpu.SemaphoreType.DMA((WPD,)), pltpu.SemaphoreType.DMA((15,)), pltpu.SemaphoreType.DMA((15,))],
        compiler_params=pltpu.CompilerParams(
            collective_id=0, has_side_effects=True, vmem_limit_bytes=40 * 2**20
        ),
        name="gather_windows",
    )(traces, live)


def scatter_kernel(
    sizes,
    flag,
    results,
    out,
    done,
    foreign,
    raw,
    early,
    late,
    side_raw,
    side_early,
    side_late,
    edge_raw,
    edge_early,
    edge_late,
    from_time,
    local_sems,
    send_sems,
    recv_sems,
):
    links = Links(sizes, send_sems, recv_sems)
    loads = [
        pltpu.make_async_copy(results.at[n], done.at[n], local_sems.at[n]) for n in range(WPD)
    ]
    for load in loads:
        load.start()
    links.barrier()
    core_i, core_x, _ = out.shape
    inner_x = pl.ds(HALO, core_x)
    sent = []

    def send(*args):
        sent.append(links.send(*args))
        return sent[-1]

    trade = links.partner(results.at[1], foreign)
    trade.start()
    for load in loads:
        load.wait()
    for h, q, span, row in pieces(WIN // HALO):
        block = done[0, span]
        lanes = lane_numbers(block.shape)
        raw[span] = jnp.where(lanes < WIN_T - HALO_T, turned(block, -HALO_T), 0.0)
        first = turned(block, q * HALO_T)
        early[row] = first if q == 0 else jnp.where(in_quarter(lanes, q), first, early[row])
    trade.wait()
    for h, q, span, row in pieces(WIN // HALO):
        block = jnp.where(flag[...][None, :1, :] > 0.5, foreign[span], done[1, span])
        lanes = lane_numbers(block.shape)
        raw[span] = raw[span] + jnp.where(lanes >= HALO_T, turned(block, HALO_T), 0.0)
        final = turned(block, q * HALO_T - (WIN_T - HALO_T))
        late[row] = final if q == 0 else jnp.where(in_quarter(lanes, q), final, late[row])

    def add(target, first, second, source):
        there = target[first, second]
        target[first, second] = there + source[...]

    waits = []
    for buffer, side in ((raw, side_raw), (early, side_early), (late, side_late)):
        whole = pl.ds(0, buffer.shape[0])
        down = send(buffer.at[whole, pl.ds(0, HALO)], side.at[0], "xl", -1)
        up = send(buffer.at[whole, pl.ds(HALO + core_x, HALO)], side.at[1], "xl", 1)
        waits += [
            (down, buffer, whole, pl.ds(core_x, HALO), side.at[0]),
            (up, buffer, whole, pl.ds(HALO, HALO), side.at[1]),
        ]

    def gathered(waits):
        for arrival, buffer, first, second, source in waits:
            links.arrive(arrival)
            _, axis, step = arrival

            @pl.when(links.has(axis, -step))
            def _():
                add(buffer, first, second, source)

    gathered(waits)

    waits = []
    for buffer, edge, width in (
        (early, edge_early, UNIT),
        (late, edge_late, UNIT),
        (raw, edge_raw, HALO),
    ):
        total = buffer.shape[0]
        inner = total - 2 * width
        down = send(buffer.at[pl.ds(0, width), inner_x], edge.at[0], "il", -1)
        up = send(buffer.at[pl.ds(total - width, width), inner_x], edge.at[1], "il", 1)
        waits += [
            (down, buffer, pl.ds(inner, width), inner_x, edge.at[0]),
            (up, buffer, pl.ds(width, width), inner_x, edge.at[1]),
        ]
    gathered(waits[:4])
    inner_p = pl.ds(UNIT, core_i // QUARTERS)
    back = send(early.at[inner_p, inner_x], from_time.at[0], "ta", -1)
    ahead = send(late.at[inner_p, inner_x], from_time.at[1], "ta", 1)
    gathered(waits[4:])
    out[...] = raw[pl.ds(HALO, core_i), inner_x]
    for arrival, side, shift in ((back, 0, WIN_T - HALO_T), (ahead, 1, 0)):
        links.arrive(arrival)
        _, axis, step = arrival

        @pl.when(links.has(axis, -step))
        def _():
            for h, q, span, row in pieces(core_i // HALO):
                block = turned(from_time[side, row], shift - q * HALO_T)
                lanes = lane_numbers(block.shape)
                kept = in_quarter(lanes, shift // HALO_T)
                out[span] = out[span] + jnp.where(kept, block, 0.0)

    links.finish(sent)


def scatter_windows(flag, done, shape, sizes):
    core_i, core_x, _ = shape
    packed = (WIN // QUARTERS, WIN, WIN_T)
    small = (WIN // QUARTERS, HALO, WIN_T)
    scratch = [
        (WPD, WIN, WIN, WIN_T),
        (WIN, WIN, WIN_T),
        (WIN, WIN, WIN_T),
        packed,
        packed,
        (2, WIN, HALO, WIN_T),
        (2,) + small,
        (2,) + small,
        (2, HALO, core_x, WIN_T),
        (2, UNIT, core_x, WIN_T),
        (2, UNIT, core_x, WIN_T),
        (2, core_i // QUARTERS, core_x, WIN_T),
    ]
    return pl.pallas_call(
        functools.partial(scatter_kernel, sizes),
        out_shape=jax.ShapeDtypeStruct(shape, jnp.float32),
        in_specs=[pl.BlockSpec(memory_space=pltpu.VMEM), pl.BlockSpec(memory_space=pl.ANY)],
        out_specs=pl.BlockSpec(memory_space=pltpu.VMEM),
        scratch_shapes=[pltpu.VMEM(shape, jnp.float32) for shape in scratch]
        + [pltpu.SemaphoreType.DMA((WPD,)), pltpu.SemaphoreType.DMA((15,)), pltpu.SemaphoreType.DMA((15,))],
        compiler_params=pltpu.CompilerParams(
            collective_id=1, has_side_effects=True, vmem_limit_bytes=40 * 2**20
        ),
        name="scatter_windows",
    )(flag, done)


def shards(sizes, traces, live, counts, levels):
    windows = gather_windows(traces, live, sizes).reshape(3, WIN * WIN, WIN_T)
    done, flag = reconstruct(windows, counts.reshape(-1), levels)
    return scatter_windows(flag, done.reshape(WPD, WIN, WIN, WIN_T), traces.shape, sizes)


def solution(mesh):
    placed = (P("il", "xl", "ta"), P("il", "xl"), P("il", None, "ta"), P())
    sizes = {axis: mesh.shape[axis] for axis in ("il", "xl", "ta")}
    return jax.shard_map(
        functools.partial(shards, sizes),
        mesh=mesh,
        in_specs=placed,
        out_specs=P("il", "xl", "ta"),
        check_vma=False,
    )
```

```python
import functools

import jax
import jax.numpy as jnp
import numpy as np
from jax import lax
from jax.experimental import pallas as pl
from jax.experimental.pallas import tpu as pltpu
from jax.sharding import PartitionSpec as P

WIN = 64
WIN_T = 128
WPD = 2
HALO = 16
HALO_T = 32
DEAD = 1e30
PITCH = 72
GROUP = 16


def cosine_table(order):
    rows = np.arange(order, dtype=np.float64)[:, None]
    columns = np.arange(order, dtype=np.float64)[None, :]
    table = np.sqrt(2.0 / order) * np.cos(np.pi * (2.0 * columns + 1.0) * rows / (2.0 * order))
    return table * np.where(rows == 0, np.sqrt(0.5), 1.0)


def taper_table(order):
    centres = np.arange(order, dtype=np.float64) + 0.5
    return np.sin(np.pi * centres / order) ** 2


def halves(table):
    high = table.astype(jnp.bfloat16)
    low = (table - high.astype(np.float64)).astype(jnp.bfloat16)
    return high, low


def tables():
    out = []
    space = cosine_table(WIN)
    for table in (space, space.T):
        high, low = halves(table)
        out.append(np.concatenate([high, high, low], axis=1))
    time = cosine_table(WIN_T)
    for table in (time.T, time):
        high, low = halves(table)
        row = np.concatenate([high, low], axis=1)
        out.append(np.concatenate([row, row], axis=0))
    plane = taper_table(WIN)[:, None] * taper_table(WIN_T)[None, :]
    lines = np.repeat(taper_table(WIN)[:, None], WIN_T, axis=1)
    return [jnp.asarray(t) for t in out] + [
        jnp.asarray(plane, jnp.float32),
        jnp.asarray(lines, jnp.float32),
    ]


def split(value):
    high = value.astype(jnp.bfloat16)
    low = (value - high.astype(jnp.float32)).astype(jnp.bfloat16)
    return high, low


def along_rows(table, slices):
    out = []
    for n in range(0, len(slices), 2):
        high, low = split(jnp.concatenate([slices[n], slices[n + 1]], axis=1))
        both = jnp.dot(
            table, jnp.concatenate([high, low, high], axis=0), preferred_element_type=jnp.float32
        )
        out += [both[:, :WIN_T], both[:, WIN_T:]]
    return out


def along_lanes(table, slices):
    high, low = split(jnp.concatenate(slices, axis=0))
    both = jnp.dot(
        jnp.concatenate([high, low], axis=1), table, preferred_element_type=jnp.float32
    )
    total = both[:, :WIN_T] + both[:, WIN_T:]
    return [total[n * WIN : (n + 1) * WIN] for n in range(len(slices))]


def shrink_kernel(
    counts,
    levels,
    windows,
    space_f,
    space_b,
    time_f,
    time_b,
    plane,
    lines,
    out,
    flag,
    held,
    window,
    ready,
    in_sems,
    out_sems,
):
    me = lax.axis_index("xl")
    other = me + 1 - 2 * lax.rem(me, 2)
    own_first, own_final = counts[WPD * me], counts[WPD * me + 1]
    other_first, other_final = counts[WPD * other], counts[WPD * other + 1]
    before = jnp.maximum(own_first + own_final, other_first + other_final)
    after = jnp.maximum(own_first + other_final, other_first + own_final)
    trading = after < before
    flag[...] = jnp.full(flag.shape, jnp.where(trading, 1.0, 0.0), jnp.float32)
    second = jnp.where(trading, 2, 1)
    pltpu.make_async_copy(windows.at[0], window.at[0], in_sems.at[0]).start()
    pltpu.make_async_copy(windows.at[second], window.at[1], in_sems.at[1]).start()

    @pl.loop(0, WPD)
    def _(slot):
        pltpu.make_async_copy(windows.at[slot], window.at[slot], in_sems.at[slot]).wait()
        final = jnp.where(trading, other_final, own_final)
        count = jnp.where(slot == 0, own_first, final)
        tables = (space_f, space_b, time_f, time_b, plane, lines)
        shrink_window(count, levels, window.at[slot], *tables, ready.at[slot], held)
        pltpu.make_async_copy(ready.at[slot], out.at[slot], out_sems.at[slot]).start()

    for slot in range(WPD):
        pltpu.make_async_copy(ready.at[slot], out.at[slot], out_sems.at[slot]).wait()


def shrink_window(
    count, levels, window, space_f, space_b, time_f, time_b, plane, lines, out, held
):
    last = count - 1

    def forward(group, estimates):
        done = along_rows(space_f[...], along_lanes(time_f[...], estimates))
        for n in range(GROUP):
            start = pl.multiple_of((group * GROUP + n) * PITCH, 8)
            held[pl.ds(start, WIN), :] = done[n]

    def recorded(group, n):
        start = pl.multiple_of((group * GROUP + n) * WIN, 8)
        return window[pl.ds(start, WIN), :]

    def backward(group):
        slices = []
        for n in range(GROUP):
            start = pl.multiple_of((group * GROUP + n) * PITCH, 8)
            slices.append(held[pl.ds(start, WIN), :])
        guesses = along_lanes(time_b[...], along_rows(space_b[...], slices))
        estimates = []
        for n in range(GROUP):
            known = recorded(group, n)
            estimates.append(jnp.where(known == DEAD, guesses[n], known))
        return estimates

    @pl.loop(0, WIN // GROUP)
    def _(group):
        estimates = []
        for n in range(GROUP):
            known = recorded(group, n)
            estimates.append(jnp.where(known == DEAD, 0.0, known))
        forward(group, estimates)

    def shrink(step):
        threshold = levels[step].astype(jnp.float32) * 0.001

        @pl.loop(0, WIN // GROUP)
        def _(group):
            first = group * GROUP
            rows = [pl.ds(first + n, WIN, stride=PITCH) for n in range(GROUP)]
            values = along_rows(space_f[...], [held[r, :] for r in rows])
            values = [v - jnp.clip(v, -threshold, threshold) for v in values]
            values = along_rows(space_b[...], values)
            for n in range(GROUP):
                held[rows[n], :] = values[n]

    @pl.loop(0, last)
    def _(step):
        shrink(step)

        @pl.loop(0, WIN // GROUP)
        def _(group):
            forward(group, backward(group))

    shrink(last)

    @pl.loop(0, WIN // GROUP)
    def _(group):
        estimates = backward(group)
        for n in range(GROUP):
            line = group * GROUP + n
            start = pl.multiple_of(line * WIN, 8)
            weight = lines[pl.ds(line, 1), :]
            out[pl.ds(start, WIN), :] = estimates[n] * (plane[...] * weight)


def reconstruct(windows, counts, levels):
    fixed = tables()
    shape = (WPD,) + windows.shape[1:]
    vmem = pl.BlockSpec(memory_space=pltpu.VMEM)
    smem = pl.BlockSpec(memory_space=pltpu.SMEM)
    hbm = pl.BlockSpec(memory_space=pl.ANY)
    return pl.pallas_call(
        shrink_kernel,
        in_specs=[smem, smem, hbm] + [vmem] * len(fixed),
        out_specs=[hbm, vmem],
        out_shape=[
            jax.ShapeDtypeStruct(shape, jnp.float32),
            jax.ShapeDtypeStruct((8, WIN_T), jnp.float32),
        ],
        scratch_shapes=[
            pltpu.VMEM((WIN * PITCH, WIN_T), jnp.float32),
            pltpu.VMEM(shape, jnp.float32),
            pltpu.VMEM(shape, jnp.float32),
            pltpu.SemaphoreType.DMA((WPD,)),
            pltpu.SemaphoreType.DMA((WPD,)),
        ],
        compiler_params=pltpu.CompilerParams(vmem_limit_bytes=40 * 2**20),
        name="shrink",
    )(counts, levels, windows, *fixed)


class Links:
    def __init__(self, sizes, send_sems, recv_sems):
        self.sizes, self.send_sems, self.recv_sems = sizes, send_sems, recv_sems
        self.me = {axis: lax.axis_index(axis) for axis in sizes}
        self.used = 0

    def has(self, axis, step):
        if step > 0:
            return self.me[axis] < self.sizes[axis] - 1
        return self.me[axis] > 0

    def barrier(self):
        barrier = pltpu.get_barrier_semaphore()
        total = 0
        for axis in self.sizes:
            for step in (-1, 1):
                there = self.has(axis, step)
                total = total + there.astype(jnp.int32)

                @pl.when(there)
                def _():
                    pl.semaphore_signal(
                        barrier,
                        inc=1,
                        device_id={axis: self.me[axis] + step},
                        device_id_type=pl.DeviceIdType.MESH,
                    )

        pl.semaphore_wait(barrier, total)

    def copy(self, source, target, axis, index):
        number = self.used
        self.used += 1
        return pltpu.make_async_remote_copy(
            src_ref=source,
            dst_ref=target,
            send_sem=self.send_sems.at[number],
            recv_sem=self.recv_sems.at[number],
            device_id={axis: index},
            device_id_type=pl.DeviceIdType.MESH,
        )

    def send(self, source, target, axis, step):
        copy = self.copy(source, target, axis, self.me[axis] + step)

        @pl.when(self.has(axis, step))
        def _():
            copy.start()

        return copy, axis, step

    def arrive(self, sent, otherwise=None):
        copy, axis, step = sent
        there = self.has(axis, -step)

        @pl.when(there)
        def _():
            copy.wait_recv()

        if otherwise is not None:

            @pl.when(jnp.logical_not(there))
            def _():
                otherwise()

    def arrive_coded(self, sent, then, otherwise=None):
        _, axis, step = sent[0]
        there = self.has(axis, -step)

        @pl.when(there)
        def _():
            for copy, _, _ in sent:
                copy.wait_recv()
            then()

        if otherwise is not None:

            @pl.when(jnp.logical_not(there))
            def _():
                otherwise()

    def finish(self, sents):
        for copy, axis, step in sents:

            @pl.when(self.has(axis, step))
            def _():
                copy.wait_send()

    def partner(self, source, target):
        me = self.me["xl"]
        return self.copy(source, target, "xl", me + 1 - 2 * lax.rem(me, 2))


QUARTERS = WIN_T // HALO_T
UNIT = HALO // QUARTERS


def lane_numbers(shape):
    return lax.broadcasted_iota(jnp.int32, shape, len(shape) - 1)


def turned(value, shift):
    shift = shift % WIN_T
    return pltpu.roll(value, shift, value.ndim - 1) if shift else value


def pieces(parts):
    for h in range(parts):
        for q in range(QUARTERS):
            start = h * HALO + q * UNIT
            yield h, q, pl.ds(start, UNIT), pl.ds(h * UNIT, UNIT)


TOP = 32767


def encode(block, words, scale, gaps):
    values = block.reshape(-1, 8, WIN_T)
    if gaps:
        gone = values == DEAD
        values = jnp.where(gone, 0.0, values)
    most = jnp.maximum(jnp.max(jnp.abs(values), axis=0), 1e-30)
    codes = jnp.round(values * (TOP / most)[None]).astype(jnp.int32)
    if gaps:
        codes = jnp.where(gone, -TOP - 1, codes)
    half = codes.shape[0] // 2
    words[...] = codes[:half] * (2 * TOP + 2) + (codes[half:] + (TOP + 1))
    scale[...] = most * (1.0 / TOP)


def decode(words, scale, shape, gaps):
    packed = words[...]
    first = packed >> 16
    second = (packed & 0xFFFF) - (TOP + 1)
    codes = jnp.concatenate([first, second], axis=0)
    values = codes.astype(jnp.float32) * scale[...][None]
    if gaps:
        values = jnp.where(codes == -TOP - 1, DEAD, values)
    return values.reshape(shape)


def code_shapes(core_x):
    tiles = core_x // 8
    large, small = HALO * tiles // 2, UNIT * tiles // 2
    words = [(2, 2, n, 8, WIN_T) for n in (large, small, small)]
    return [pltpu.VMEM(w, jnp.int32) for w in words] + [
        pltpu.VMEM((2, 2, 3, 8, WIN_T), jnp.float32)
    ]


class Coder:
    def __init__(self, send, words, scales, gaps):
        self.send, self.words, self.scales, self.gaps = send, words, scales, gaps

    def put(self, block, kind, side):
        words, scale = self.words[kind], self.scales
        encode(block, words.at[0, side], scale.at[0, side, kind], self.gaps)

    def go(self, kind, side):
        words, scale = self.words[kind], self.scales
        step = 2 * side - 1
        return (
            self.send(words.at[0, side], words.at[1, side], "il", step),
            self.send(scale.at[0, side, kind], scale.at[1, side, kind], "il", step),
        )

    def get(self, kind, side, shape):
        words, scale = self.words[kind], self.scales
        return decode(words.at[1, side], scale.at[1, side, kind], shape, self.gaps)


def in_quarter(lanes, q):
    return (lanes >= q * HALO_T) & (lanes < (q + 1) * HALO_T)


def gather_kernel(
    sizes,
    traces,
    live,
    out,
    mine,
    raw,
    early,
    late,
    to_next,
    to_prev,
    ready,
    words_raw,
    words_early,
    words_late,
    scales,
    local_sems,
    send_sems,
    recv_sems,
):
    links = Links(sizes, send_sems, recv_sems)
    core_i, core_x, _ = mine.shape
    square = (core_x, core_x)
    same = lax.broadcasted_iota(jnp.int32, square, 0) == lax.broadcasted_iota(jnp.int32, square, 1)
    spread = [jnp.where(same, live[pl.ds(n, 1), :], 0) for n in range(core_i)]
    spread = jnp.concatenate(spread, axis=0).astype(jnp.float32).astype(jnp.bfloat16)
    ones = jnp.ones((core_x, WIN_T), jnp.bfloat16)
    seen = jnp.dot(spread, ones, preferred_element_type=jnp.float32).reshape(mine.shape)
    mine[...] = jnp.where(seen > 0.5, traces[...], DEAD)
    inner_x = pl.ds(HALO, core_x)
    low_i, high_i = pl.ds(0, HALO), pl.ds(HALO + core_i, HALO)
    sent = []

    def send(*args):
        sent.append(links.send(*args))
        return sent[-1]

    coder = Coder(send, (words_raw, words_early, words_late), scales, True)
    coder.put(mine[pl.ds(0, HALO)], 0, 0)
    coder.put(mine[pl.ds(core_i - HALO, HALO)], 0, 1)
    links.barrier()
    waits = [(coder.go(0, 0), raw, 0, 0, high_i), (coder.go(0, 1), raw, 0, 1, low_i)]

    for h, q, span, row in pieces(core_i // HALO):
        block = mine[span]
        lanes = lane_numbers(block.shape)
        chosen = in_quarter(lanes, q)
        first = turned(block, q * HALO_T)
        final = turned(block, q * HALO_T - (WIN_T - HALO_T))
        to_prev[row] = first if q == 0 else jnp.where(chosen, first, to_prev[row])
        to_next[row] = final if q == 0 else jnp.where(chosen, final, to_next[row])

    inner_p = pl.ds(UNIT, core_i // QUARTERS)
    early_in = send(to_next, early.at[inner_p, inner_x], "ta", 1)
    late_in = send(to_prev, late.at[inner_p, inner_x], "ta", -1)
    raw[pl.ds(HALO, core_i), inner_x] = mine[...]

    def blank(target, source):
        def fill():
            target[inner_p, inner_x] = jnp.where(source[...] == DEAD, DEAD, 0.0)

        return fill

    low_p, high_p = pl.ds(0, UNIT), pl.ds(UNIT + core_i // QUARTERS, UNIT)
    from_p = pl.ds(core_i // QUARTERS, UNIT)
    for arrival, buffer, source, kind in (
        (early_in, early, to_next, 1),
        (late_in, late, to_prev, 2),
    ):
        links.arrive(arrival, blank(buffer, source))
        coder.put(buffer[pl.ds(UNIT, UNIT), inner_x], kind, 0)
        coder.put(buffer[from_p, inner_x], kind, 1)
        waits += [
            (coder.go(kind, 0), buffer, kind, 0, high_p),
            (coder.go(kind, 1), buffer, kind, 1, low_p),
        ]

    def missing(target, first, second):
        def fill():
            shape = target.at[first, second].shape
            target[first, second] = jnp.full(shape, DEAD, jnp.float32)

        return fill

    def restored(target, kind, side, first):
        def fill():
            shape = target.at[first, inner_x].shape
            target[first, inner_x] = coder.get(kind, side, shape)

        return fill

    for arrival, buffer, kind, side, place in waits:
        links.arrive_coded(
            arrival, restored(buffer, kind, side, place), missing(buffer, place, inner_x)
        )

    waits = []
    low_x, high_x = pl.ds(0, HALO), pl.ds(HALO + core_x, HALO)
    for buffer in (raw, early, late):
        whole = pl.ds(0, buffer.shape[0])
        up = send(buffer.at[whole, pl.ds(core_x, HALO)], buffer.at[whole, low_x], "xl", 1)
        down = send(buffer.at[whole, pl.ds(HALO, HALO)], buffer.at[whole, high_x], "xl", -1)
        waits += [(up, buffer, low_x), (down, buffer, high_x)]
    for arrival, buffer, place in waits:
        links.arrive(arrival, missing(buffer, pl.ds(0, buffer.shape[0]), place))

    trades = []
    for h, q, span, row in pieces(WIN // HALO):
        block = raw[span]
        lanes = lane_numbers(block.shape)
        added = turned(late[row], WIN_T - HALO_T - q * HALO_T)
        ready[1, span] = jnp.where(lanes < WIN_T - HALO_T, turned(block, -HALO_T), added)
        if q == QUARTERS - 1:
            part = pl.ds(h * HALO, HALO)
            trades.append(links.partner(ready.at[1, part], out.at[2, part]))
            trades[-1].start()
    keep = [pltpu.make_async_copy(ready.at[n], out.at[n], local_sems.at[n]) for n in range(WPD)]
    keep[1].start()
    for h, q, span, row in pieces(WIN // HALO):
        block = raw[span]
        lanes = lane_numbers(block.shape)
        added = turned(early[row], -q * HALO_T)
        ready[0, span] = jnp.where(lanes < HALO_T, added, turned(block, HALO_T))
    keep[0].start()
    keep[0].wait()
    keep[1].wait()
    for trade in trades:
        trade.wait()
    links.finish(sent)


def gather_windows(traces, live, sizes):
    packed = (WIN // QUARTERS, WIN, WIN_T)
    small = (traces.shape[0] // QUARTERS, traces.shape[1], WIN_T)
    scratch = [traces.shape, (WIN, WIN, WIN_T), packed, packed, small, small]
    scratch += [(WPD, WIN, WIN, WIN_T)]
    codes = code_shapes(traces.shape[1])
    return pl.pallas_call(
        functools.partial(gather_kernel, sizes),
        out_shape=jax.ShapeDtypeStruct((3, WIN, WIN, WIN_T), jnp.float32),
        in_specs=[pl.BlockSpec(memory_space=pltpu.VMEM)] * 2,
        out_specs=pl.BlockSpec(memory_space=pl.ANY),
        scratch_shapes=[pltpu.VMEM(shape, jnp.float32) for shape in scratch]
        + codes
        + [pltpu.SemaphoreType.DMA((n,)) for n in (WPD, 24, 24)],
        compiler_params=pltpu.CompilerParams(
            collective_id=0, has_side_effects=True, vmem_limit_bytes=40 * 2**20
        ),
        name="gather_windows",
    )(traces, live)


def scatter_kernel(
    sizes,
    flag,
    results,
    out,
    done,
    foreign,
    raw,
    early,
    late,
    side_raw,
    side_early,
    side_late,
    words_raw,
    words_early,
    words_late,
    scales,
    from_time,
    local_sems,
    send_sems,
    recv_sems,
):
    links = Links(sizes, send_sems, recv_sems)
    loads = [
        pltpu.make_async_copy(results.at[n], done.at[n], local_sems.at[n]) for n in range(WPD)
    ]
    for load in loads:
        load.start()
    links.barrier()
    core_i, core_x, _ = out.shape
    inner_x = pl.ds(HALO, core_x)
    sent = []

    def send(*args):
        sent.append(links.send(*args))
        return sent[-1]

    parts = [pl.ds(h * HALO, HALO) for h in range(WIN // HALO)]
    trades = [links.partner(results.at[1, part], foreign.at[part]) for part in parts]
    for trade in trades:
        trade.start()
    for load in loads:
        load.wait()
    for h, q, span, row in pieces(WIN // HALO):
        block = done[0, span]
        lanes = lane_numbers(block.shape)
        raw[span] = jnp.where(lanes < WIN_T - HALO_T, turned(block, -HALO_T), 0.0)
        first = turned(block, q * HALO_T)
        early[row] = first if q == 0 else jnp.where(in_quarter(lanes, q), first, early[row])
    for h, q, span, row in pieces(WIN // HALO):
        if q == 0:
            trades[h].wait()
        block = jnp.where(flag[...][None, :1, :] > 0.5, foreign[span], done[1, span])
        lanes = lane_numbers(block.shape)
        raw[span] = raw[span] + jnp.where(lanes >= HALO_T, turned(block, HALO_T), 0.0)
        final = turned(block, q * HALO_T - (WIN_T - HALO_T))
        late[row] = final if q == 0 else jnp.where(in_quarter(lanes, q), final, late[row])

    def add(target, first, second, source):
        there = target[first, second]
        target[first, second] = there + source[...]

    waits = []
    for buffer, side in ((raw, side_raw), (early, side_early), (late, side_late)):
        whole = pl.ds(0, buffer.shape[0])
        down = send(buffer.at[whole, pl.ds(0, HALO)], side.at[0], "xl", -1)
        up = send(buffer.at[whole, pl.ds(HALO + core_x, HALO)], side.at[1], "xl", 1)
        waits += [
            (down, buffer, whole, pl.ds(core_x, HALO), side.at[0]),
            (up, buffer, whole, pl.ds(HALO, HALO), side.at[1]),
        ]

    def gathered(waits):
        for arrival, buffer, first, second, source in waits:
            links.arrive(arrival)
            _, axis, step = arrival

            @pl.when(links.has(axis, -step))
            def _():
                add(buffer, first, second, source)

    gathered(waits)

    coder = Coder(send, (words_raw, words_early, words_late), scales, False)
    waits = []
    for buffer, kind, width in ((early, 1, UNIT), (late, 2, UNIT), (raw, 0, HALO)):
        total = buffer.shape[0]
        inner = total - 2 * width
        coder.put(buffer[pl.ds(0, width), inner_x], kind, 0)
        coder.put(buffer[pl.ds(total - width, width), inner_x], kind, 1)
        waits += [
            (coder.go(kind, 0), buffer, kind, 0, pl.ds(inner, width)),
            (coder.go(kind, 1), buffer, kind, 1, pl.ds(width, width)),
        ]

    def added(target, kind, side, first):
        def fill():
            there = target[first, inner_x]
            target[first, inner_x] = there + coder.get(kind, side, there.shape)

        return fill

    for arrival, buffer, kind, side, place in waits[:4]:
        links.arrive_coded(arrival, added(buffer, kind, side, place))
    inner_p = pl.ds(UNIT, core_i // QUARTERS)
    back = send(early.at[inner_p, inner_x], from_time.at[0], "ta", -1)
    ahead = send(late.at[inner_p, inner_x], from_time.at[1], "ta", 1)
    for arrival, buffer, kind, side, place in waits[4:]:
        links.arrive_coded(arrival, added(buffer, kind, side, place))
    out[...] = raw[pl.ds(HALO, core_i), inner_x]
    for arrival, side, shift in ((back, 0, WIN_T - HALO_T), (ahead, 1, 0)):
        links.arrive(arrival)
        _, axis, step = arrival

        @pl.when(links.has(axis, -step))
        def _():
            for h, q, span, row in pieces(core_i // HALO):
                block = turned(from_time[side, row], shift - q * HALO_T)
                lanes = lane_numbers(block.shape)
                kept = in_quarter(lanes, shift // HALO_T)
                out[span] = out[span] + jnp.where(kept, block, 0.0)

    links.finish(sent)


def scatter_windows(flag, done, shape, sizes):
    core_i, core_x, _ = shape
    packed = (WIN // QUARTERS, WIN, WIN_T)
    small = (WIN // QUARTERS, HALO, WIN_T)
    scratch = [
        (WPD, WIN, WIN, WIN_T),
        (WIN, WIN, WIN_T),
        (WIN, WIN, WIN_T),
        packed,
        packed,
        (2, WIN, HALO, WIN_T),
        (2,) + small,
        (2,) + small,
    ]
    time_side = pltpu.VMEM((2, core_i // QUARTERS, core_x, WIN_T), jnp.float32)
    codes = code_shapes(core_x) + [time_side]
    return pl.pallas_call(
        functools.partial(scatter_kernel, sizes),
        out_shape=jax.ShapeDtypeStruct(shape, jnp.float32),
        in_specs=[pl.BlockSpec(memory_space=pltpu.VMEM), pl.BlockSpec(memory_space=pl.ANY)],
        out_specs=pl.BlockSpec(memory_space=pltpu.VMEM),
        scratch_shapes=[pltpu.VMEM(shape, jnp.float32) for shape in scratch]
        + codes
        + [pltpu.SemaphoreType.DMA((n,)) for n in (WPD, 24, 24)],
        compiler_params=pltpu.CompilerParams(
            collective_id=1, has_side_effects=True, vmem_limit_bytes=40 * 2**20
        ),
        name="scatter_windows",
    )(flag, done)


def shards(sizes, traces, live, counts, levels):
    windows = gather_windows(traces, live, sizes).reshape(3, WIN * WIN, WIN_T)
    done, flag = reconstruct(windows, counts.reshape(-1), levels)
    return scatter_windows(flag, done.reshape(WPD, WIN, WIN, WIN_T), traces.shape, sizes)


def solution(mesh):
    placed = (P("il", "xl", "ta"), P("il", "xl"), P("il", None, "ta"), P())
    sizes = {axis: mesh.shape[axis] for axis in ("il", "xl", "ta")}
    return jax.shard_map(
        functools.partial(shards, sizes),
        mesh=mesh,
        in_specs=placed,
        out_specs=P("il", "xl", "ta"),
        check_vma=False,
    )
```

```python
import functools

import jax
import jax.numpy as jnp
import numpy as np
from jax import lax
from jax.experimental import pallas as pl
from jax.experimental.pallas import tpu as pltpu
from jax.sharding import PartitionSpec as P

WIN = 64
WIN_T = 128
WPD = 2
HALO = 16
HALO_T = 32
DEAD = 1e30
PITCH = 72
GROUP = 32
CHUNK = GROUP * WIN
CHUNKS = WIN // GROUP


def cosine_table(order):
    rows = np.arange(order, dtype=np.float64)[:, None]
    columns = np.arange(order, dtype=np.float64)[None, :]
    table = np.sqrt(2.0 / order) * np.cos(np.pi * (2.0 * columns + 1.0) * rows / (2.0 * order))
    return table * np.where(rows == 0, np.sqrt(0.5), 1.0)


def taper_table(order):
    centres = np.arange(order, dtype=np.float64) + 0.5
    return np.sin(np.pi * centres / order) ** 2


def halves(table):
    high = table.astype(jnp.bfloat16)
    low = (table - high.astype(np.float64)).astype(jnp.bfloat16)
    return high, low


def tables():
    out = []
    space = cosine_table(WIN)
    for table in (space, space.T):
        high, low = halves(table)
        out.append(np.concatenate([high, high, low], axis=1))
    time = cosine_table(WIN_T)
    for table in (time.T, time):
        high, low = halves(table)
        row = np.concatenate([high, low], axis=1)
        out.append(np.concatenate([row, row], axis=0))
    plane = taper_table(WIN)[:, None] * taper_table(WIN_T)[None, :]
    lines = np.repeat(taper_table(WIN)[:, None], WIN_T, axis=1)
    return [jnp.asarray(t) for t in out] + [
        jnp.asarray(plane, jnp.float32),
        jnp.asarray(lines, jnp.float32),
    ]


def split(value):
    high = value.astype(jnp.bfloat16)
    low = (value - high.astype(jnp.float32)).astype(jnp.bfloat16)
    return high, low


def along_rows(table, slices):
    out = []
    for n in range(0, len(slices), 2):
        high, low = split(jnp.concatenate([slices[n], slices[n + 1]], axis=1))
        both = jnp.dot(
            table, jnp.concatenate([high, low, high], axis=0), preferred_element_type=jnp.float32
        )
        out += [both[:, :WIN_T], both[:, WIN_T:]]
    return out


def along_lanes(table, slices):
    high, low = split(jnp.concatenate(slices, axis=0))
    both = jnp.dot(
        jnp.concatenate([high, low], axis=1), table, preferred_element_type=jnp.float32
    )
    total = both[:, :WIN_T] + both[:, WIN_T:]
    return [total[n * WIN : (n + 1) * WIN] for n in range(len(slices))]


def shrink_kernel(
    counts,
    levels,
    windows,
    space_f,
    space_b,
    time_f,
    time_b,
    plane,
    lines,
    out,
    flag,
    held,
    window,
    ready,
    in_sems,
    out_sems,
):
    me = lax.axis_index("xl")
    other = me + 1 - 2 * lax.rem(me, 2)
    own_first, own_final = counts[0, me, 0], counts[0, me, WPD - 1]
    other_first, other_final = counts[0, other, 0], counts[0, other, WPD - 1]
    before = jnp.maximum(own_first + own_final, other_first + other_final)
    after = jnp.maximum(own_first + other_final, other_first + own_final)
    trading = after < before
    flag[...] = jnp.full(flag.shape, jnp.where(trading, 1.0, 0.0), jnp.float32)
    second = jnp.where(trading, 2, 1)

    def load(slot, source, chunk):
        rows = pl.ds(chunk * CHUNK, CHUNK)
        return pltpu.make_async_copy(
            windows.at[source, rows], window.at[slot, rows], in_sems.at[slot, chunk]
        )

    def store(slot, chunk):
        rows = pl.ds(chunk * CHUNK, CHUNK)
        return pltpu.make_async_copy(
            ready.at[slot, rows], out.at[slot, rows], out_sems.at[slot, chunk]
        )

    for slot, source in enumerate((0, second)):
        for chunk in range(CHUNKS):
            load(slot, source, chunk).start()

    @pl.loop(0, WPD)
    def _(slot):
        final = jnp.where(trading, other_final, own_final)
        count = jnp.where(slot == 0, own_first, final)
        tables = (space_f, space_b, time_f, time_b, plane, lines)
        shrink_window(
            count,
            levels,
            window.at[slot],
            *tables,
            ready.at[slot],
            held,
            lambda group: load(slot, slot, group).wait(),
            lambda group: store(slot, group).start(),
        )

    for slot in range(WPD):
        for chunk in range(CHUNKS):
            store(slot, chunk).wait()


def shrink_window(
    count,
    levels,
    window,
    space_f,
    space_b,
    time_f,
    time_b,
    plane,
    lines,
    out,
    held,
    take,
    give,
):
    last = count - 1

    def forward(group, estimates):
        done = along_rows(space_f[...], along_lanes(time_f[...], estimates))
        for n in range(GROUP):
            start = pl.multiple_of((group * GROUP + n) * PITCH, 8)
            held[pl.ds(start, WIN), :] = done[n]

    def recorded(group, n):
        start = pl.multiple_of((group * GROUP + n) * WIN, 8)
        return window[pl.ds(start, WIN), :]

    def backward(group):
        slices = []
        for n in range(GROUP):
            start = pl.multiple_of((group * GROUP + n) * PITCH, 8)
            slices.append(held[pl.ds(start, WIN), :])
        guesses = along_lanes(time_b[...], along_rows(space_b[...], slices))
        estimates = []
        for n in range(GROUP):
            known = recorded(group, n)
            estimates.append(jnp.where(known == DEAD, guesses[n], known))
        return estimates

    @pl.loop(0, WIN // GROUP)
    def _(group):
        take(group)
        estimates = []
        for n in range(GROUP):
            known = recorded(group, n)
            estimates.append(jnp.where(known == DEAD, 0.0, known))
        forward(group, estimates)

    def shrink(step):
        threshold = levels[step].astype(jnp.float32) * 0.001

        @pl.loop(0, WIN // GROUP)
        def _(group):
            first = group * GROUP
            rows = [pl.ds(first + n, WIN, stride=PITCH) for n in range(GROUP)]
            values = along_rows(space_f[...], [held[r, :] for r in rows])
            values = [v - jnp.clip(v, -threshold, threshold) for v in values]
            values = along_rows(space_b[...], values)
            for n in range(GROUP):
                held[rows[n], :] = values[n]

    @pl.loop(0, last)
    def _(step):
        shrink(step)

        @pl.loop(0, WIN // GROUP)
        def _(group):
            forward(group, backward(group))

    shrink(last)

    @pl.loop(0, WIN // GROUP)
    def _(group):
        estimates = backward(group)
        for n in range(GROUP):
            line = group * GROUP + n
            start = pl.multiple_of(line * WIN, 8)
            weight = lines[pl.ds(line, 1), :]
            out[pl.ds(start, WIN), :] = estimates[n] * (plane[...] * weight)
        give(group)


def reconstruct(windows, counts, levels):
    fixed = tables()
    shape = (WPD,) + windows.shape[1:]
    vmem = pl.BlockSpec(memory_space=pltpu.VMEM)
    smem = pl.BlockSpec(memory_space=pltpu.SMEM)
    hbm = pl.BlockSpec(memory_space=pl.ANY)
    return pl.pallas_call(
        shrink_kernel,
        in_specs=[smem, smem, hbm] + [vmem] * len(fixed),
        out_specs=[hbm, vmem],
        out_shape=[
            jax.ShapeDtypeStruct(shape, jnp.float32),
            jax.ShapeDtypeStruct((8, WIN_T), jnp.float32),
        ],
        scratch_shapes=[
            pltpu.VMEM((WIN * PITCH, WIN_T), jnp.float32),
            pltpu.VMEM(shape, jnp.float32),
            pltpu.VMEM(shape, jnp.float32),
            pltpu.SemaphoreType.DMA((WPD, CHUNKS)),
            pltpu.SemaphoreType.DMA((WPD, CHUNKS)),
        ],
        compiler_params=pltpu.CompilerParams(vmem_limit_bytes=40 * 2**20),
        name="shrink",
    )(counts, levels, windows, *fixed)


class Links:
    def __init__(self, sizes, send_sems, recv_sems):
        self.sizes, self.send_sems, self.recv_sems = sizes, send_sems, recv_sems
        self.me = {axis: lax.axis_index(axis) for axis in sizes}
        self.used = 0

    def has(self, axis, step):
        if step > 0:
            return self.me[axis] < self.sizes[axis] - 1
        return self.me[axis] > 0

    def greet(self):
        barrier = pltpu.get_barrier_semaphore()
        total = 0
        for axis in self.sizes:
            for step in (-1, 1):
                there = self.has(axis, step)
                total = total + there.astype(jnp.int32)

                @pl.when(there)
                def _():
                    pl.semaphore_signal(
                        barrier,
                        inc=1,
                        device_id={axis: self.me[axis] + step},
                        device_id_type=pl.DeviceIdType.MESH,
                    )

        return barrier, total

    def barrier(self):
        barrier, total = self.greet()
        pl.semaphore_wait(barrier, total)

    def copy(self, source, target, axis, index):
        number = self.used
        self.used += 1
        return pltpu.make_async_remote_copy(
            src_ref=source,
            dst_ref=target,
            send_sem=self.send_sems.at[number],
            recv_sem=self.recv_sems.at[number],
            device_id={axis: index},
            device_id_type=pl.DeviceIdType.MESH,
        )

    def send(self, source, target, axis, step):
        copy = self.copy(source, target, axis, self.me[axis] + step)

        @pl.when(self.has(axis, step))
        def _():
            copy.start()

        return copy, axis, step

    def arrive(self, sent, otherwise=None):
        copy, axis, step = sent
        there = self.has(axis, -step)

        @pl.when(there)
        def _():
            copy.wait_recv()

        if otherwise is not None:

            @pl.when(jnp.logical_not(there))
            def _():
                otherwise()

    def arrive_coded(self, sent, then, otherwise=None):
        _, axis, step = sent[0]
        there = self.has(axis, -step)

        @pl.when(there)
        def _():
            for copy, _, _ in sent:
                copy.wait_recv()
            then()

        if otherwise is not None:

            @pl.when(jnp.logical_not(there))
            def _():
                otherwise()

    def finish(self, sents):
        for copy, axis, step in sents:

            @pl.when(self.has(axis, step))
            def _():
                copy.wait_send()

    def partner(self, source, target):
        me = self.me["xl"]
        return self.copy(source, target, "xl", me + 1 - 2 * lax.rem(me, 2))


QUARTERS = WIN_T // HALO_T
UNIT = HALO // QUARTERS


def lane_numbers(shape):
    return lax.broadcasted_iota(jnp.int32, shape, len(shape) - 1)


def turned(value, shift):
    shift = shift % WIN_T
    return pltpu.roll(value, shift, value.ndim - 1) if shift else value


def pieces(parts):
    for h in range(parts):
        for q in range(QUARTERS):
            start = h * HALO + q * UNIT
            yield h, q, pl.ds(start, UNIT), pl.ds(h * UNIT, UNIT)


TOP = 32767


def encode(block, words, scale, gaps):
    values = block.reshape(-1, 8, WIN_T)
    if gaps:
        gone = values == DEAD
        values = jnp.where(gone, 0.0, values)
    most = jnp.maximum(jnp.max(jnp.abs(values), axis=0), 1e-30)
    codes = jnp.round(values * (TOP / most)[None]).astype(jnp.int32)
    if gaps:
        codes = jnp.where(gone, -TOP - 1, codes)
    half = codes.shape[0] // 2
    words[...] = codes[:half] * (2 * TOP + 2) + (codes[half:] + (TOP + 1))
    scale[...] = most * (1.0 / TOP)


def decode(words, scale, shape, gaps):
    packed = words[...]
    first = packed >> 16
    second = (packed & 0xFFFF) - (TOP + 1)
    codes = jnp.concatenate([first, second], axis=0)
    values = codes.astype(jnp.float32) * scale[...][None]
    if gaps:
        values = jnp.where(codes == -TOP - 1, DEAD, values)
    return values.reshape(shape)


def code_shapes(core_x):
    tiles = core_x // 8
    large, small = HALO * tiles // 2, UNIT * tiles // 2
    words = [(2, 2, n, 8, WIN_T) for n in (large, small, small)]
    return [pltpu.VMEM(w, jnp.int32) for w in words] + [
        pltpu.VMEM((2, 2, 3, 8, WIN_T), jnp.float32)
    ]


class Coder:
    def __init__(self, send, words, scales, gaps):
        self.send, self.words, self.scales, self.gaps = send, words, scales, gaps

    def put(self, block, kind, side):
        words, scale = self.words[kind], self.scales
        encode(block, words.at[0, side], scale.at[0, side, kind], self.gaps)

    def go(self, kind, side):
        words, scale = self.words[kind], self.scales
        step = 2 * side - 1
        return (
            self.send(words.at[0, side], words.at[1, side], "il", step),
            self.send(scale.at[0, side, kind], scale.at[1, side, kind], "il", step),
        )

    def get(self, kind, side, shape):
        words, scale = self.words[kind], self.scales
        return decode(words.at[1, side], scale.at[1, side, kind], shape, self.gaps)


def in_quarter(lanes, q):
    return (lanes >= q * HALO_T) & (lanes < (q + 1) * HALO_T)


def gather_kernel(
    sizes,
    traces,
    live,
    out,
    mine,
    raw,
    early,
    late,
    to_next,
    to_prev,
    ready,
    words_raw,
    words_early,
    words_late,
    scales,
    local_sems,
    send_sems,
    recv_sems,
):
    links = Links(sizes, send_sems, recv_sems)
    core_i, core_x, _ = mine.shape
    own = pltpu.make_async_copy(traces, mine, local_sems.at[0])
    own.start()
    barrier, total = links.greet()
    square = (core_x, core_x)
    same = lax.broadcasted_iota(jnp.int32, square, 0) == lax.broadcasted_iota(jnp.int32, square, 1)
    spread = [jnp.where(same, live[pl.ds(n, 1), :], 0) for n in range(core_i)]
    spread = jnp.concatenate(spread, axis=0).astype(jnp.float32).astype(jnp.bfloat16)
    ones = jnp.ones((core_x, WIN_T), jnp.bfloat16)
    seen = jnp.dot(spread, ones, preferred_element_type=jnp.float32).reshape(mine.shape)
    own.wait()
    mine[...] = jnp.where(seen > 0.5, mine[...], DEAD)
    inner_x = pl.ds(HALO, core_x)
    low_i, high_i = pl.ds(0, HALO), pl.ds(HALO + core_i, HALO)
    sent = []

    def send(*args):
        sent.append(links.send(*args))
        return sent[-1]

    coder = Coder(send, (words_raw, words_early, words_late), scales, True)
    coder.put(mine[pl.ds(0, HALO)], 0, 0)
    coder.put(mine[pl.ds(core_i - HALO, HALO)], 0, 1)
    pl.semaphore_wait(barrier, total)
    waits = [(coder.go(0, 0), raw, 0, 0, high_i), (coder.go(0, 1), raw, 0, 1, low_i)]

    for h, q, span, row in pieces(core_i // HALO):
        block = mine[span]
        lanes = lane_numbers(block.shape)
        chosen = in_quarter(lanes, q)
        first = turned(block, q * HALO_T)
        final = turned(block, q * HALO_T - (WIN_T - HALO_T))
        to_prev[row] = first if q == 0 else jnp.where(chosen, first, to_prev[row])
        to_next[row] = final if q == 0 else jnp.where(chosen, final, to_next[row])

    inner_p = pl.ds(UNIT, core_i // QUARTERS)
    early_in = send(to_next, early.at[inner_p, inner_x], "ta", 1)
    late_in = send(to_prev, late.at[inner_p, inner_x], "ta", -1)
    raw[pl.ds(HALO, core_i), inner_x] = mine[...]

    def blank(target, source):
        def fill():
            target[inner_p, inner_x] = jnp.where(source[...] == DEAD, DEAD, 0.0)

        return fill

    low_p, high_p = pl.ds(0, UNIT), pl.ds(UNIT + core_i // QUARTERS, UNIT)
    from_p = pl.ds(core_i // QUARTERS, UNIT)
    for arrival, buffer, source, kind in (
        (early_in, early, to_next, 1),
        (late_in, late, to_prev, 2),
    ):
        links.arrive(arrival, blank(buffer, source))
        coder.put(buffer[pl.ds(UNIT, UNIT), inner_x], kind, 0)
        coder.put(buffer[from_p, inner_x], kind, 1)
        waits += [
            (coder.go(kind, 0), buffer, kind, 0, high_p),
            (coder.go(kind, 1), buffer, kind, 1, low_p),
        ]

    def missing(target, first, second):
        def fill():
            shape = target.at[first, second].shape
            target[first, second] = jnp.full(shape, DEAD, jnp.float32)

        return fill

    def restored(target, kind, side, first):
        def fill():
            shape = target.at[first, inner_x].shape
            target[first, inner_x] = coder.get(kind, side, shape)

        return fill

    for arrival, buffer, kind, side, place in waits:
        links.arrive_coded(
            arrival, restored(buffer, kind, side, place), missing(buffer, place, inner_x)
        )

    waits = []
    low_x, high_x = pl.ds(0, HALO), pl.ds(HALO + core_x, HALO)
    for buffer in (raw, early, late):
        whole = pl.ds(0, buffer.shape[0])
        up = send(buffer.at[whole, pl.ds(core_x, HALO)], buffer.at[whole, low_x], "xl", 1)
        down = send(buffer.at[whole, pl.ds(HALO, HALO)], buffer.at[whole, high_x], "xl", -1)
        waits += [(up, buffer, low_x), (down, buffer, high_x)]
    for arrival, buffer, place in waits:
        links.arrive(arrival, missing(buffer, pl.ds(0, buffer.shape[0]), place))

    trades = []
    for h, q, span, row in pieces(WIN // HALO):
        block = raw[span]
        lanes = lane_numbers(block.shape)
        added = turned(late[row], WIN_T - HALO_T - q * HALO_T)
        ready[1, span] = jnp.where(lanes < WIN_T - HALO_T, turned(block, -HALO_T), added)
        if q == QUARTERS - 1:
            part = pl.ds(h * HALO, HALO)
            trades.append(links.partner(ready.at[1, part], out.at[2, part]))
            trades[-1].start()
    keep = [pltpu.make_async_copy(ready.at[n], out.at[n], local_sems.at[n]) for n in range(WPD)]
    keep[1].start()
    for h, q, span, row in pieces(WIN // HALO):
        block = raw[span]
        lanes = lane_numbers(block.shape)
        added = turned(early[row], -q * HALO_T)
        ready[0, span] = jnp.where(lanes < HALO_T, added, turned(block, HALO_T))
    keep[0].start()
    keep[0].wait()
    keep[1].wait()
    for trade in trades:
        trade.wait()
    links.finish(sent)


def gather_windows(traces, live, sizes):
    packed = (WIN // QUARTERS, WIN, WIN_T)
    small = (traces.shape[0] // QUARTERS, traces.shape[1], WIN_T)
    scratch = [traces.shape, (WIN, WIN, WIN_T), packed, packed, small, small]
    scratch += [(WPD, WIN, WIN, WIN_T)]
    codes = code_shapes(traces.shape[1])
    return pl.pallas_call(
        functools.partial(gather_kernel, sizes),
        out_shape=jax.ShapeDtypeStruct((3, WIN, WIN, WIN_T), jnp.float32),
        in_specs=[
            pl.BlockSpec(memory_space=pl.ANY),
            pl.BlockSpec(memory_space=pltpu.VMEM),
        ],
        out_specs=pl.BlockSpec(memory_space=pl.ANY),
        scratch_shapes=[pltpu.VMEM(shape, jnp.float32) for shape in scratch]
        + codes
        + [pltpu.SemaphoreType.DMA((n,)) for n in (WPD, 24, 24)],
        compiler_params=pltpu.CompilerParams(
            collective_id=0, has_side_effects=True, vmem_limit_bytes=40 * 2**20
        ),
        name="gather_windows",
    )(traces, live)


def scatter_kernel(
    sizes,
    flag,
    results,
    out,
    done,
    foreign,
    raw,
    early,
    late,
    side_raw,
    side_early,
    side_late,
    words_raw,
    words_early,
    words_late,
    scales,
    from_time,
    local_sems,
    send_sems,
    recv_sems,
):
    links = Links(sizes, send_sems, recv_sems)
    loads = [
        pltpu.make_async_copy(results.at[n], done.at[n], local_sems.at[n]) for n in range(WPD)
    ]
    for load in loads:
        load.start()
    links.barrier()
    core_i, core_x, _ = out.shape
    inner_x = pl.ds(HALO, core_x)
    sent = []

    def send(*args):
        sent.append(links.send(*args))
        return sent[-1]

    parts = [pl.ds(h * HALO, HALO) for h in range(WIN // HALO)]
    trades = [links.partner(results.at[1, part], foreign.at[part]) for part in parts]
    for trade in trades:
        trade.start()
    for load in loads:
        load.wait()
    for h, q, span, row in pieces(WIN // HALO):
        block = done[0, span]
        lanes = lane_numbers(block.shape)
        raw[span] = jnp.where(lanes < WIN_T - HALO_T, turned(block, -HALO_T), 0.0)
        first = turned(block, q * HALO_T)
        early[row] = first if q == 0 else jnp.where(in_quarter(lanes, q), first, early[row])
    for h, q, span, row in pieces(WIN // HALO):
        if q == 0:
            trades[h].wait()
        block = jnp.where(flag[...][None, :1, :] > 0.5, foreign[span], done[1, span])
        lanes = lane_numbers(block.shape)
        raw[span] = raw[span] + jnp.where(lanes >= HALO_T, turned(block, HALO_T), 0.0)
        final = turned(block, q * HALO_T - (WIN_T - HALO_T))
        late[row] = final if q == 0 else jnp.where(in_quarter(lanes, q), final, late[row])

    def add(target, first, second, source):
        there = target[first, second]
        target[first, second] = there + source[...]

    waits = []
    for buffer, side in ((raw, side_raw), (early, side_early), (late, side_late)):
        whole = pl.ds(0, buffer.shape[0])
        down = send(buffer.at[whole, pl.ds(0, HALO)], side.at[0], "xl", -1)
        up = send(buffer.at[whole, pl.ds(HALO + core_x, HALO)], side.at[1], "xl", 1)
        waits += [
            (down, buffer, whole, pl.ds(core_x, HALO), side.at[0]),
            (up, buffer, whole, pl.ds(HALO, HALO), side.at[1]),
        ]

    def gathered(waits):
        for arrival, buffer, first, second, source in waits:
            links.arrive(arrival)
            _, axis, step = arrival

            @pl.when(links.has(axis, -step))
            def _():
                add(buffer, first, second, source)

    gathered(waits)

    coder = Coder(send, (words_raw, words_early, words_late), scales, False)
    waits = []
    for buffer, kind, width in ((early, 1, UNIT), (late, 2, UNIT), (raw, 0, HALO)):
        total = buffer.shape[0]
        inner = total - 2 * width
        coder.put(buffer[pl.ds(0, width), inner_x], kind, 0)
        coder.put(buffer[pl.ds(total - width, width), inner_x], kind, 1)
        waits += [
            (coder.go(kind, 0), buffer, kind, 0, pl.ds(inner, width)),
            (coder.go(kind, 1), buffer, kind, 1, pl.ds(width, width)),
        ]

    def added(target, kind, side, first):
        def fill():
            there = target[first, inner_x]
            target[first, inner_x] = there + coder.get(kind, side, there.shape)

        return fill

    for arrival, buffer, kind, side, place in waits[:4]:
        links.arrive_coded(arrival, added(buffer, kind, side, place))
    inner_p = pl.ds(UNIT, core_i // QUARTERS)
    back = send(early.at[inner_p, inner_x], from_time.at[0], "ta", -1)
    ahead = send(late.at[inner_p, inner_x], from_time.at[1], "ta", 1)
    for arrival, buffer, kind, side, place in waits[4:]:
        links.arrive_coded(arrival, added(buffer, kind, side, place))
    out[...] = raw[pl.ds(HALO, core_i), inner_x]
    for arrival, side, shift in ((back, 0, WIN_T - HALO_T), (ahead, 1, 0)):
        links.arrive(arrival)
        _, axis, step = arrival

        @pl.when(links.has(axis, -step))
        def _():
            for h, q, span, row in pieces(core_i // HALO):
                block = turned(from_time[side, row], shift - q * HALO_T)
                lanes = lane_numbers(block.shape)
                kept = in_quarter(lanes, shift // HALO_T)
                out[span] = out[span] + jnp.where(kept, block, 0.0)

    links.finish(sent)


def scatter_windows(flag, done, shape, sizes):
    core_i, core_x, _ = shape
    packed = (WIN // QUARTERS, WIN, WIN_T)
    small = (WIN // QUARTERS, HALO, WIN_T)
    scratch = [
        (WPD, WIN, WIN, WIN_T),
        (WIN, WIN, WIN_T),
        (WIN, WIN, WIN_T),
        packed,
        packed,
        (2, WIN, HALO, WIN_T),
        (2,) + small,
        (2,) + small,
    ]
    time_side = pltpu.VMEM((2, core_i // QUARTERS, core_x, WIN_T), jnp.float32)
    codes = code_shapes(core_x) + [time_side]
    return pl.pallas_call(
        functools.partial(scatter_kernel, sizes),
        out_shape=jax.ShapeDtypeStruct(shape, jnp.float32),
        in_specs=[pl.BlockSpec(memory_space=pltpu.VMEM), pl.BlockSpec(memory_space=pl.ANY)],
        out_specs=pl.BlockSpec(memory_space=pltpu.VMEM),
        scratch_shapes=[pltpu.VMEM(shape, jnp.float32) for shape in scratch]
        + codes
        + [pltpu.SemaphoreType.DMA((n,)) for n in (WPD, 24, 24)],
        compiler_params=pltpu.CompilerParams(
            collective_id=1, has_side_effects=True, vmem_limit_bytes=40 * 2**20
        ),
        name="scatter_windows",
    )(flag, done)


def shards(sizes, traces, live, counts, levels):
    windows = gather_windows(traces, live, sizes).reshape(3, WIN * WIN, WIN_T)
    done, flag = reconstruct(windows, counts, levels)
    return scatter_windows(flag, done.reshape(WPD, WIN, WIN, WIN_T), traces.shape, sizes)


def solution(mesh):
    placed = (P("il", "xl", "ta"), P("il", "xl"), P("il", None, "ta"), P())
    sizes = {axis: mesh.shape[axis] for axis in ("il", "xl", "ta")}
    return jax.shard_map(
        functools.partial(shards, sizes),
        mesh=mesh,
        in_specs=placed,
        out_specs=P("il", "xl", "ta"),
        check_vma=False,
    )
```

```python
import functools

import jax
import jax.numpy as jnp
import numpy as np
from jax import lax
from jax.experimental import pallas as pl
from jax.experimental.pallas import tpu as pltpu
from jax.sharding import PartitionSpec as P

WIN = 64
WIN_T = 128
WPD = 2
HALO = 16
HALO_T = 32
DEAD = 1e30
PITCH = 72
GROUP = 64
PIECE = 16
CHUNK = PIECE * WIN
CHUNKS = WIN // PIECE


def cosine_table(order):
    rows = np.arange(order, dtype=np.float64)[:, None]
    columns = np.arange(order, dtype=np.float64)[None, :]
    table = np.sqrt(2.0 / order) * np.cos(np.pi * (2.0 * columns + 1.0) * rows / (2.0 * order))
    return table * np.where(rows == 0, np.sqrt(0.5), 1.0)


def taper_table(order):
    centres = np.arange(order, dtype=np.float64) + 0.5
    return np.sin(np.pi * centres / order) ** 2


def halves(table):
    high = table.astype(jnp.bfloat16)
    low = (table - high.astype(np.float64)).astype(jnp.bfloat16)
    return high, low


def tables():
    out = []
    space = cosine_table(WIN)
    for table in (space, space.T):
        high, low = halves(table)
        out.append(np.concatenate([high, high, low], axis=1))
    time = cosine_table(WIN_T)
    for table in (time.T, time):
        high, low = halves(table)
        row = np.concatenate([high, low], axis=1)
        out.append(np.concatenate([row, row], axis=0))
    plane = taper_table(WIN)[:, None] * taper_table(WIN_T)[None, :]
    lines = np.repeat(taper_table(WIN)[:, None], WIN_T, axis=1)
    return [jnp.asarray(t) for t in out] + [
        jnp.asarray(plane, jnp.float32),
        jnp.asarray(lines, jnp.float32),
    ]


def split(value):
    high = value.astype(jnp.bfloat16)
    low = (value - high.astype(jnp.float32)).astype(jnp.bfloat16)
    return high, low


def along_rows(table, slices):
    out = []
    for n in range(0, len(slices), 2):
        high, low = split(jnp.concatenate([slices[n], slices[n + 1]], axis=1))
        both = jnp.dot(
            table, jnp.concatenate([high, low, high], axis=0), preferred_element_type=jnp.float32
        )
        out += [both[:, :WIN_T], both[:, WIN_T:]]
    return out


def along_lanes(table, slices):
    high, low = split(jnp.concatenate(slices, axis=0))
    both = jnp.dot(
        jnp.concatenate([high, low], axis=1), table, preferred_element_type=jnp.float32
    )
    total = both[:, :WIN_T] + both[:, WIN_T:]
    return [total[n * WIN : (n + 1) * WIN] for n in range(len(slices))]


def shrink_kernel(
    counts,
    levels,
    windows,
    space_f,
    space_b,
    time_f,
    time_b,
    plane,
    lines,
    out,
    flag,
    held,
    window,
    ready,
    in_sems,
    out_sems,
):
    me = lax.axis_index("xl")
    other = me + 1 - 2 * lax.rem(me, 2)
    own_first, own_final = counts[0, me, 0], counts[0, me, WPD - 1]
    other_first, other_final = counts[0, other, 0], counts[0, other, WPD - 1]
    before = jnp.maximum(own_first + own_final, other_first + other_final)
    after = jnp.maximum(own_first + other_final, other_first + own_final)
    trading = after < before
    flag[...] = jnp.full(flag.shape, jnp.where(trading, 1.0, 0.0), jnp.float32)
    second = jnp.where(trading, 2, 1)

    def load(slot, source, chunk):
        rows = pl.ds(chunk * CHUNK, CHUNK)
        return pltpu.make_async_copy(
            windows.at[source, rows], window.at[slot, rows], in_sems.at[slot, chunk]
        )

    def store(slot, chunk):
        rows = pl.ds(chunk * CHUNK, CHUNK)
        return pltpu.make_async_copy(
            ready.at[slot, rows], out.at[slot, rows], out_sems.at[slot, chunk]
        )

    for slot, source in enumerate((0, second)):
        for chunk in range(CHUNKS):
            load(slot, source, chunk).start()

    @pl.loop(0, WPD)
    def _(slot):
        final = jnp.where(trading, other_final, own_final)
        count = jnp.where(slot == 0, own_first, final)
        tables = (space_f, space_b, time_f, time_b, plane, lines)
        shrink_window(
            count,
            levels,
            window.at[slot],
            *tables,
            ready.at[slot],
            held,
            lambda chunk: load(slot, slot, chunk).wait(),
            lambda chunk: store(slot, chunk).start(),
        )

    for slot in range(WPD):
        for chunk in range(CHUNKS):
            store(slot, chunk).wait()


def shrink_window(
    count,
    levels,
    window,
    space_f,
    space_b,
    time_f,
    time_b,
    plane,
    lines,
    out,
    held,
    take,
    give,
):
    last = count - 1

    def forward(group, estimates):
        done = along_rows(space_f[...], along_lanes(time_f[...], estimates))
        for n in range(GROUP):
            start = pl.multiple_of((group * GROUP + n) * PITCH, 8)
            held[pl.ds(start, WIN), :] = done[n]

    def recorded(group, n):
        start = pl.multiple_of((group * GROUP + n) * WIN, 8)
        return window[pl.ds(start, WIN), :]

    def backward(group):
        slices = []
        for n in range(GROUP):
            start = pl.multiple_of((group * GROUP + n) * PITCH, 8)
            slices.append(held[pl.ds(start, WIN), :])
        guesses = along_lanes(time_b[...], along_rows(space_b[...], slices))
        estimates = []
        for n in range(GROUP):
            known = recorded(group, n)
            estimates.append(jnp.where(known == DEAD, guesses[n], known))
        return estimates

    @pl.loop(0, WIN // GROUP)
    def _(group):
        estimates = []
        for n in range(GROUP):
            if n % PIECE == 0:
                take(group * (GROUP // PIECE) + n // PIECE)
            known = recorded(group, n)
            estimates.append(jnp.where(known == DEAD, 0.0, known))
        forward(group, estimates)

    def shrink(step):
        threshold = levels[step].astype(jnp.float32) * 0.001

        @pl.loop(0, WIN // GROUP)
        def _(group):
            first = group * GROUP
            rows = [pl.ds(first + n, WIN, stride=PITCH) for n in range(GROUP)]
            values = along_rows(space_f[...], [held[r, :] for r in rows])
            values = [v - jnp.clip(v, -threshold, threshold) for v in values]
            values = along_rows(space_b[...], values)
            for n in range(GROUP):
                held[rows[n], :] = values[n]

    @pl.loop(0, last)
    def _(step):
        shrink(step)

        @pl.loop(0, WIN // GROUP)
        def _(group):
            forward(group, backward(group))

    shrink(last)

    @pl.loop(0, WIN // GROUP)
    def _(group):
        estimates = backward(group)
        for n in range(GROUP):
            line = group * GROUP + n
            start = pl.multiple_of(line * WIN, 8)
            weight = lines[pl.ds(line, 1), :]
            out[pl.ds(start, WIN), :] = estimates[n] * (plane[...] * weight)
            if n % PIECE == PIECE - 1:
                give(group * (GROUP // PIECE) + n // PIECE)


def reconstruct(windows, counts, levels):
    fixed = tables()
    shape = (WPD,) + windows.shape[1:]
    vmem = pl.BlockSpec(memory_space=pltpu.VMEM)
    smem = pl.BlockSpec(memory_space=pltpu.SMEM)
    hbm = pl.BlockSpec(memory_space=pl.ANY)
    return pl.pallas_call(
        shrink_kernel,
        in_specs=[smem, smem, hbm] + [vmem] * len(fixed),
        out_specs=[hbm, vmem],
        out_shape=[
            jax.ShapeDtypeStruct(shape, jnp.float32),
            jax.ShapeDtypeStruct((8, WIN_T), jnp.float32),
        ],
        scratch_shapes=[
            pltpu.VMEM((WIN * PITCH, WIN_T), jnp.float32),
            pltpu.VMEM(shape, jnp.float32),
            pltpu.VMEM(shape, jnp.float32),
            pltpu.SemaphoreType.DMA((WPD, CHUNKS)),
            pltpu.SemaphoreType.DMA((WPD, CHUNKS)),
        ],
        compiler_params=pltpu.CompilerParams(vmem_limit_bytes=40 * 2**20),
        name="shrink",
    )(counts, levels, windows, *fixed)


class Links:
    def __init__(self, sizes, send_sems, recv_sems):
        self.sizes, self.send_sems, self.recv_sems = sizes, send_sems, recv_sems
        self.me = {axis: lax.axis_index(axis) for axis in sizes}
        self.used = 0

    def has(self, axis, step):
        if step > 0:
            return self.me[axis] < self.sizes[axis] - 1
        return self.me[axis] > 0

    def greet(self):
        barrier = pltpu.get_barrier_semaphore()
        total = 0
        for axis in self.sizes:
            for step in (-1, 1):
                there = self.has(axis, step)
                total = total + there.astype(jnp.int32)

                @pl.when(there)
                def _():
                    pl.semaphore_signal(
                        barrier,
                        inc=1,
                        device_id={axis: self.me[axis] + step},
                        device_id_type=pl.DeviceIdType.MESH,
                    )

        return barrier, total

    def barrier(self):
        barrier, total = self.greet()
        pl.semaphore_wait(barrier, total)

    def copy(self, source, target, axis, index):
        number = self.used
        self.used += 1
        return pltpu.make_async_remote_copy(
            src_ref=source,
            dst_ref=target,
            send_sem=self.send_sems.at[number],
            recv_sem=self.recv_sems.at[number],
            device_id={axis: index},
            device_id_type=pl.DeviceIdType.MESH,
        )

    def send(self, source, target, axis, step):
        copy = self.copy(source, target, axis, self.me[axis] + step)

        @pl.when(self.has(axis, step))
        def _():
            copy.start()

        return copy, axis, step

    def arrive(self, sent, otherwise=None):
        copy, axis, step = sent
        there = self.has(axis, -step)

        @pl.when(there)
        def _():
            copy.wait_recv()

        if otherwise is not None:

            @pl.when(jnp.logical_not(there))
            def _():
                otherwise()

    def arrive_coded(self, sent, then, otherwise=None):
        _, axis, step = sent[0]
        there = self.has(axis, -step)

        @pl.when(there)
        def _():
            for copy, _, _ in sent:
                copy.wait_recv()
            then()

        if otherwise is not None:

            @pl.when(jnp.logical_not(there))
            def _():
                otherwise()

    def finish(self, sents):
        for copy, axis, step in sents:

            @pl.when(self.has(axis, step))
            def _():
                copy.wait_send()

    def partner(self, source, target):
        me = self.me["xl"]
        return self.copy(source, target, "xl", me + 1 - 2 * lax.rem(me, 2))


QUARTERS = WIN_T // HALO_T
UNIT = HALO // QUARTERS


def lane_numbers(shape):
    return lax.broadcasted_iota(jnp.int32, shape, len(shape) - 1)


def turned(value, shift):
    shift = shift % WIN_T
    return pltpu.roll(value, shift, value.ndim - 1) if shift else value


def pieces(parts):
    for h in range(parts):
        for q in range(QUARTERS):
            start = h * HALO + q * UNIT
            yield h, q, pl.ds(start, UNIT), pl.ds(h * UNIT, UNIT)


TOP = 32767


def encode(block, words, scale, gaps):
    values = block.reshape(-1, 8, WIN_T)
    if gaps:
        gone = values == DEAD
        values = jnp.where(gone, 0.0, values)
    most = jnp.maximum(jnp.max(jnp.abs(values), axis=0), 1e-30)
    codes = jnp.round(values * (TOP / most)[None]).astype(jnp.int32)
    if gaps:
        codes = jnp.where(gone, -TOP - 1, codes)
    half = codes.shape[0] // 2
    words[...] = codes[:half] * (2 * TOP + 2) + (codes[half:] + (TOP + 1))
    scale[...] = most * (1.0 / TOP)


def decode(words, scale, shape, gaps):
    packed = words[...]
    first = packed >> 16
    second = (packed & 0xFFFF) - (TOP + 1)
    codes = jnp.concatenate([first, second], axis=0)
    values = codes.astype(jnp.float32) * scale[...][None]
    if gaps:
        values = jnp.where(codes == -TOP - 1, DEAD, values)
    return values.reshape(shape)


def code_shapes(core_x):
    tiles = core_x // 8
    large, small = HALO * tiles // 2, UNIT * tiles // 2
    words = [(2, 2, n, 8, WIN_T) for n in (large, small, small)]
    return [pltpu.VMEM(w, jnp.int32) for w in words] + [
        pltpu.VMEM((2, 2, 3, 8, WIN_T), jnp.float32)
    ]


class Coder:
    def __init__(self, send, words, scales, gaps):
        self.send, self.words, self.scales, self.gaps = send, words, scales, gaps

    def put(self, block, kind, side):
        words, scale = self.words[kind], self.scales
        encode(block, words.at[0, side], scale.at[0, side, kind], self.gaps)

    def go(self, kind, side):
        words, scale = self.words[kind], self.scales
        step = 2 * side - 1
        return (
            self.send(words.at[0, side], words.at[1, side], "il", step),
            self.send(scale.at[0, side, kind], scale.at[1, side, kind], "il", step),
        )

    def get(self, kind, side, shape):
        words, scale = self.words[kind], self.scales
        return decode(words.at[1, side], scale.at[1, side, kind], shape, self.gaps)


def in_quarter(lanes, q):
    return (lanes >= q * HALO_T) & (lanes < (q + 1) * HALO_T)


def gather_kernel(
    sizes,
    traces,
    flags,
    out,
    mine,
    live,
    raw,
    early,
    late,
    to_next,
    to_prev,
    ready,
    words_raw,
    words_early,
    words_late,
    scales,
    local_sems,
    send_sems,
    recv_sems,
):
    links = Links(sizes, send_sems, recv_sems)
    core_i, core_x, _ = mine.shape
    own = pltpu.make_async_copy(traces, mine, local_sems.at[0])
    own.start()
    known = pltpu.make_async_copy(flags, live, local_sems.at[1])
    known.start()
    barrier, total = links.greet()
    known.wait()
    square = (core_x, core_x)
    same = lax.broadcasted_iota(jnp.int32, square, 0) == lax.broadcasted_iota(jnp.int32, square, 1)
    spread = [jnp.where(same, live[pl.ds(n, 1), :], 0) for n in range(core_i)]
    spread = jnp.concatenate(spread, axis=0).astype(jnp.float32).astype(jnp.bfloat16)
    ones = jnp.ones((core_x, WIN_T), jnp.bfloat16)
    seen = jnp.dot(spread, ones, preferred_element_type=jnp.float32).reshape(mine.shape)
    own.wait()
    mine[...] = jnp.where(seen > 0.5, mine[...], DEAD)
    inner_x = pl.ds(HALO, core_x)
    low_i, high_i = pl.ds(0, HALO), pl.ds(HALO + core_i, HALO)
    sent = []

    def send(*args):
        sent.append(links.send(*args))
        return sent[-1]

    coder = Coder(send, (words_raw, words_early, words_late), scales, True)
    coder.put(mine[pl.ds(0, HALO)], 0, 0)
    coder.put(mine[pl.ds(core_i - HALO, HALO)], 0, 1)
    pl.semaphore_wait(barrier, total)
    waits = [(coder.go(0, 0), raw, 0, 0, high_i), (coder.go(0, 1), raw, 0, 1, low_i)]

    for h, q, span, row in pieces(core_i // HALO):
        block = mine[span]
        lanes = lane_numbers(block.shape)
        chosen = in_quarter(lanes, q)
        first = turned(block, q * HALO_T)
        final = turned(block, q * HALO_T - (WIN_T - HALO_T))
        to_prev[row] = first if q == 0 else jnp.where(chosen, first, to_prev[row])
        to_next[row] = final if q == 0 else jnp.where(chosen, final, to_next[row])

    inner_p = pl.ds(UNIT, core_i // QUARTERS)
    early_in = send(to_next, early.at[inner_p, inner_x], "ta", 1)
    late_in = send(to_prev, late.at[inner_p, inner_x], "ta", -1)
    raw[pl.ds(HALO, core_i), inner_x] = mine[...]

    def blank(target, source):
        def fill():
            target[inner_p, inner_x] = jnp.where(source[...] == DEAD, DEAD, 0.0)

        return fill

    low_p, high_p = pl.ds(0, UNIT), pl.ds(UNIT + core_i // QUARTERS, UNIT)
    from_p = pl.ds(core_i // QUARTERS, UNIT)
    for arrival, buffer, source, kind in (
        (early_in, early, to_next, 1),
        (late_in, late, to_prev, 2),
    ):
        links.arrive(arrival, blank(buffer, source))
        coder.put(buffer[pl.ds(UNIT, UNIT), inner_x], kind, 0)
        coder.put(buffer[from_p, inner_x], kind, 1)
        waits += [
            (coder.go(kind, 0), buffer, kind, 0, high_p),
            (coder.go(kind, 1), buffer, kind, 1, low_p),
        ]

    def missing(target, first, second):
        def fill():
            shape = target.at[first, second].shape
            target[first, second] = jnp.full(shape, DEAD, jnp.float32)

        return fill

    def restored(target, kind, side, first):
        def fill():
            shape = target.at[first, inner_x].shape
            target[first, inner_x] = coder.get(kind, side, shape)

        return fill

    for arrival, buffer, kind, side, place in waits:
        links.arrive_coded(
            arrival, restored(buffer, kind, side, place), missing(buffer, place, inner_x)
        )

    waits = []
    low_x, high_x = pl.ds(0, HALO), pl.ds(HALO + core_x, HALO)
    for buffer in (raw, early, late):
        whole = pl.ds(0, buffer.shape[0])
        up = send(buffer.at[whole, pl.ds(core_x, HALO)], buffer.at[whole, low_x], "xl", 1)
        down = send(buffer.at[whole, pl.ds(HALO, HALO)], buffer.at[whole, high_x], "xl", -1)
        waits += [(up, buffer, low_x), (down, buffer, high_x)]
    for arrival, buffer, place in waits:
        links.arrive(arrival, missing(buffer, pl.ds(0, buffer.shape[0]), place))

    trades = []
    for h, q, span, row in pieces(WIN // HALO):
        block = raw[span]
        lanes = lane_numbers(block.shape)
        added = turned(late[row], WIN_T - HALO_T - q * HALO_T)
        ready[1, span] = jnp.where(lanes < WIN_T - HALO_T, turned(block, -HALO_T), added)
        if q == QUARTERS - 1:
            part = pl.ds(h * HALO, HALO)
            trades.append(links.partner(ready.at[1, part], out.at[2, part]))
            trades[-1].start()
    keep = [pltpu.make_async_copy(ready.at[n], out.at[n], local_sems.at[n]) for n in range(WPD)]
    keep[1].start()
    for h, q, span, row in pieces(WIN // HALO):
        block = raw[span]
        lanes = lane_numbers(block.shape)
        added = turned(early[row], -q * HALO_T)
        ready[0, span] = jnp.where(lanes < HALO_T, added, turned(block, HALO_T))
    keep[0].start()
    keep[0].wait()
    keep[1].wait()
    for trade in trades:
        trade.wait()
    links.finish(sent)


def gather_windows(traces, live, sizes):
    packed = (WIN // QUARTERS, WIN, WIN_T)
    small = (traces.shape[0] // QUARTERS, traces.shape[1], WIN_T)
    scratch = [traces.shape, (WIN, WIN, WIN_T), packed, packed, small, small]
    scratch += [(WPD, WIN, WIN, WIN_T)]
    codes = code_shapes(traces.shape[1])
    return pl.pallas_call(
        functools.partial(gather_kernel, sizes),
        out_shape=jax.ShapeDtypeStruct((3, WIN, WIN, WIN_T), jnp.float32),
        in_specs=[
            pl.BlockSpec(memory_space=pltpu.HBM),
            pl.BlockSpec(memory_space=pltpu.HBM),
        ],
        out_specs=pl.BlockSpec(memory_space=pl.ANY),
        scratch_shapes=[pltpu.VMEM(traces.shape, jnp.float32), pltpu.VMEM(live.shape, jnp.int32)]
        + [pltpu.VMEM(shape, jnp.float32) for shape in scratch[1:]]
        + codes
        + [pltpu.SemaphoreType.DMA((n,)) for n in (WPD, 24, 24)],
        compiler_params=pltpu.CompilerParams(
            collective_id=0, has_side_effects=True, vmem_limit_bytes=40 * 2**20
        ),
        name="gather_windows",
    )(traces, live)


def scatter_kernel(
    sizes,
    flag,
    results,
    out,
    done,
    foreign,
    raw,
    early,
    late,
    side_raw,
    side_early,
    side_late,
    words_raw,
    words_early,
    words_late,
    scales,
    from_time,
    local_sems,
    send_sems,
    recv_sems,
):
    links = Links(sizes, send_sems, recv_sems)
    loads = [
        pltpu.make_async_copy(results.at[n], done.at[n], local_sems.at[n]) for n in range(WPD)
    ]
    for load in loads:
        load.start()
    links.barrier()
    core_i, core_x, _ = out.shape
    inner_x = pl.ds(HALO, core_x)
    sent = []

    def send(*args):
        sent.append(links.send(*args))
        return sent[-1]

    parts = [pl.ds(h * HALO, HALO) for h in range(WIN // HALO)]
    trades = [links.partner(results.at[1, part], foreign.at[part]) for part in parts]
    for trade in trades:
        trade.start()
    for load in loads:
        load.wait()
    for h, q, span, row in pieces(WIN // HALO):
        block = done[0, span]
        lanes = lane_numbers(block.shape)
        raw[span] = jnp.where(lanes < WIN_T - HALO_T, turned(block, -HALO_T), 0.0)
        first = turned(block, q * HALO_T)
        early[row] = first if q == 0 else jnp.where(in_quarter(lanes, q), first, early[row])
    for h, q, span, row in pieces(WIN // HALO):
        if q == 0:
            trades[h].wait()
        block = jnp.where(flag[...][None, :1, :] > 0.5, foreign[span], done[1, span])
        lanes = lane_numbers(block.shape)
        raw[span] = raw[span] + jnp.where(lanes >= HALO_T, turned(block, HALO_T), 0.0)
        final = turned(block, q * HALO_T - (WIN_T - HALO_T))
        late[row] = final if q == 0 else jnp.where(in_quarter(lanes, q), final, late[row])

    def add(target, first, second, source):
        there = target[first, second]
        target[first, second] = there + source[...]

    waits = []
    for buffer, side in ((raw, side_raw), (early, side_early), (late, side_late)):
        whole = pl.ds(0, buffer.shape[0])
        down = send(buffer.at[whole, pl.ds(0, HALO)], side.at[0], "xl", -1)
        up = send(buffer.at[whole, pl.ds(HALO + core_x, HALO)], side.at[1], "xl", 1)
        waits += [
            (down, buffer, whole, pl.ds(core_x, HALO), side.at[0]),
            (up, buffer, whole, pl.ds(HALO, HALO), side.at[1]),
        ]

    def gathered(waits):
        for arrival, buffer, first, second, source in waits:
            links.arrive(arrival)
            _, axis, step = arrival

            @pl.when(links.has(axis, -step))
            def _():
                add(buffer, first, second, source)

    gathered(waits)

    coder = Coder(send, (words_raw, words_early, words_late), scales, False)
    waits = []
    for buffer, kind, width in ((early, 1, UNIT), (late, 2, UNIT), (raw, 0, HALO)):
        total = buffer.shape[0]
        inner = total - 2 * width
        coder.put(buffer[pl.ds(0, width), inner_x], kind, 0)
        coder.put(buffer[pl.ds(total - width, width), inner_x], kind, 1)
        waits += [
            (coder.go(kind, 0), buffer, kind, 0, pl.ds(inner, width)),
            (coder.go(kind, 1), buffer, kind, 1, pl.ds(width, width)),
        ]

    def added(target, kind, side, first):
        def fill():
            there = target[first, inner_x]
            target[first, inner_x] = there + coder.get(kind, side, there.shape)

        return fill

    for arrival, buffer, kind, side, place in waits[:4]:
        links.arrive_coded(arrival, added(buffer, kind, side, place))
    inner_p = pl.ds(UNIT, core_i // QUARTERS)
    back = send(early.at[inner_p, inner_x], from_time.at[0], "ta", -1)
    ahead = send(late.at[inner_p, inner_x], from_time.at[1], "ta", 1)
    for arrival, buffer, kind, side, place in waits[4:]:
        links.arrive_coded(arrival, added(buffer, kind, side, place))
    out[...] = raw[pl.ds(HALO, core_i), inner_x]
    for arrival, side, shift in ((back, 0, WIN_T - HALO_T), (ahead, 1, 0)):
        links.arrive(arrival)
        _, axis, step = arrival

        @pl.when(links.has(axis, -step))
        def _():
            for h, q, span, row in pieces(core_i // HALO):
                block = turned(from_time[side, row], shift - q * HALO_T)
                lanes = lane_numbers(block.shape)
                kept = in_quarter(lanes, shift // HALO_T)
                out[span] = out[span] + jnp.where(kept, block, 0.0)

    links.finish(sent)


def scatter_windows(flag, done, shape, sizes):
    core_i, core_x, _ = shape
    packed = (WIN // QUARTERS, WIN, WIN_T)
    small = (WIN // QUARTERS, HALO, WIN_T)
    scratch = [
        (WPD, WIN, WIN, WIN_T),
        (WIN, WIN, WIN_T),
        (WIN, WIN, WIN_T),
        packed,
        packed,
        (2, WIN, HALO, WIN_T),
        (2,) + small,
        (2,) + small,
    ]
    time_side = pltpu.VMEM((2, core_i // QUARTERS, core_x, WIN_T), jnp.float32)
    codes = code_shapes(core_x) + [time_side]
    return pl.pallas_call(
        functools.partial(scatter_kernel, sizes),
        out_shape=jax.ShapeDtypeStruct(shape, jnp.float32),
        in_specs=[pl.BlockSpec(memory_space=pltpu.VMEM), pl.BlockSpec(memory_space=pl.ANY)],
        out_specs=pl.BlockSpec(memory_space=pltpu.VMEM),
        scratch_shapes=[pltpu.VMEM(shape, jnp.float32) for shape in scratch]
        + codes
        + [pltpu.SemaphoreType.DMA((n,)) for n in (WPD, 24, 24)],
        compiler_params=pltpu.CompilerParams(
            collective_id=1, has_side_effects=True, vmem_limit_bytes=40 * 2**20
        ),
        name="scatter_windows",
    )(flag, done)


def shards(sizes, traces, live, counts, levels):
    windows = gather_windows(traces, live, sizes).reshape(3, WIN * WIN, WIN_T)
    done, flag = reconstruct(windows, counts, levels)
    return scatter_windows(flag, done.reshape(WPD, WIN, WIN, WIN_T), traces.shape, sizes)


def solution(mesh):
    placed = (P("il", "xl", "ta"), P("il", "xl"), P("il", None, "ta"), P())
    sizes = {axis: mesh.shape[axis] for axis in ("il", "xl", "ta")}
    return jax.shard_map(
        functools.partial(shards, sizes),
        mesh=mesh,
        in_specs=placed,
        out_specs=P("il", "xl", "ta"),
        check_vma=False,
    )
```

```python
import functools

import jax
import jax.numpy as jnp
import numpy as np
from jax import lax
from jax.experimental import pallas as pl
from jax.experimental.pallas import tpu as pltpu
from jax.sharding import PartitionSpec as P

WIN = 64
WIN_T = 128
WPD = 2
HALO = 16
HALO_T = 32
DEAD = 1e30
PITCH = 72
GROUP = 64
PIECE = 16
CHUNK = PIECE * WIN
CHUNKS = WIN // PIECE


def cosine_table(order):
    rows = np.arange(order, dtype=np.float64)[:, None]
    columns = np.arange(order, dtype=np.float64)[None, :]
    table = np.sqrt(2.0 / order) * np.cos(np.pi * (2.0 * columns + 1.0) * rows / (2.0 * order))
    return table * np.where(rows == 0, np.sqrt(0.5), 1.0)


def taper_table(order):
    centres = np.arange(order, dtype=np.float64) + 0.5
    return np.sin(np.pi * centres / order) ** 2


def halves(table):
    high = table.astype(jnp.bfloat16)
    low = (table - high.astype(np.float64)).astype(jnp.bfloat16)
    return high, low


def tables():
    out = []
    space = cosine_table(WIN)
    for table in (space, space.T):
        high, low = halves(table)
        out.append(np.concatenate([high, high, low], axis=1))
    time = cosine_table(WIN_T)
    for table in (time.T, time):
        high, low = halves(table)
        row = np.concatenate([high, low], axis=1)
        out.append(np.concatenate([row, row], axis=0))
    plane = taper_table(WIN)[:, None] * taper_table(WIN_T)[None, :]
    lines = np.repeat(taper_table(WIN)[:, None], WIN_T, axis=1)
    return [jnp.asarray(t) for t in out] + [
        jnp.asarray(plane, jnp.float32),
        jnp.asarray(lines, jnp.float32),
    ]


def split(value):
    high = value.astype(jnp.bfloat16)
    low = (value - high.astype(jnp.float32)).astype(jnp.bfloat16)
    return high, low


def along_rows(table, slices):
    out = []
    for n in range(0, len(slices), 2):
        high, low = split(jnp.concatenate([slices[n], slices[n + 1]], axis=1))
        both = jnp.dot(
            table, jnp.concatenate([high, low, high], axis=0), preferred_element_type=jnp.float32
        )
        out += [both[:, :WIN_T], both[:, WIN_T:]]
    return out


def along_lanes(table, slices):
    high, low = split(jnp.concatenate(slices, axis=0))
    both = jnp.dot(
        jnp.concatenate([high, low], axis=1), table, preferred_element_type=jnp.float32
    )
    total = both[:, :WIN_T] + both[:, WIN_T:]
    return [total[n * WIN : (n + 1) * WIN] for n in range(len(slices))]


def shrink_kernel(
    counts,
    levels,
    windows,
    space_f,
    space_b,
    time_f,
    time_b,
    plane,
    lines,
    out,
    flag,
    held,
    window,
    ready,
    in_sems,
    out_sems,
):
    me = lax.axis_index("xl")
    other = me + 1 - 2 * lax.rem(me, 2)
    own_first, own_final = counts[0, me, 0], counts[0, me, WPD - 1]
    other_first, other_final = counts[0, other, 0], counts[0, other, WPD - 1]
    before = jnp.maximum(own_first + own_final, other_first + other_final)
    after = jnp.maximum(own_first + other_final, other_first + own_final)
    trading = after < before
    flag[...] = jnp.full(flag.shape, jnp.where(trading, 1.0, 0.0), jnp.float32)
    second = jnp.where(trading, 2, 1)

    def load(slot, source, chunk):
        rows = pl.ds(chunk * CHUNK, CHUNK)
        return pltpu.make_async_copy(
            windows.at[source, rows], window.at[slot, rows], in_sems.at[slot, chunk]
        )

    def store(slot, chunk):
        rows = pl.ds(chunk * CHUNK, CHUNK)
        return pltpu.make_async_copy(
            ready.at[slot, rows], out.at[slot, rows], out_sems.at[slot, chunk]
        )

    for slot, source in enumerate((0, second)):
        for chunk in range(CHUNKS):
            load(slot, source, chunk).start()

    @pl.loop(0, WPD)
    def _(slot):
        final = jnp.where(trading, other_final, own_final)
        count = jnp.where(slot == 0, own_first, final)
        tables = (space_f, space_b, time_f, time_b, plane, lines)
        shrink_window(
            count,
            levels,
            window.at[slot],
            *tables,
            ready.at[slot],
            held,
            lambda chunk: load(slot, slot, chunk).wait(),
            lambda chunk: store(slot, chunk).start(),
        )

    for slot in range(WPD):
        for chunk in range(CHUNKS):
            store(slot, chunk).wait()


def shrink_window(
    count,
    levels,
    window,
    space_f,
    space_b,
    time_f,
    time_b,
    plane,
    lines,
    out,
    held,
    take,
    give,
):
    last = count - 1

    def forward(group, estimates):
        done = along_rows(space_f[...], along_lanes(time_f[...], estimates))
        for n in range(GROUP):
            start = pl.multiple_of((group * GROUP + n) * PITCH, 8)
            held[pl.ds(start, WIN), :] = done[n]

    def recorded(group, n):
        start = pl.multiple_of((group * GROUP + n) * WIN, 8)
        return window[pl.ds(start, WIN), :]

    def backward(group):
        slices = []
        for n in range(GROUP):
            start = pl.multiple_of((group * GROUP + n) * PITCH, 8)
            slices.append(held[pl.ds(start, WIN), :])
        guesses = along_lanes(time_b[...], along_rows(space_b[...], slices))
        estimates = []
        for n in range(GROUP):
            known = recorded(group, n)
            estimates.append(jnp.where(known == DEAD, guesses[n], known))
        return estimates

    @pl.loop(0, WIN // GROUP)
    def _(group):
        estimates = []
        for n in range(GROUP):
            if n % PIECE == 0:
                take(group * (GROUP // PIECE) + n // PIECE)
            known = recorded(group, n)
            estimates.append(jnp.where(known == DEAD, 0.0, known))
        forward(group, estimates)

    def shrink(step):
        threshold = levels[step].astype(jnp.float32) * 0.001

        @pl.loop(0, WIN // GROUP)
        def _(group):
            first = group * GROUP
            rows = [pl.ds(first + n, WIN, stride=PITCH) for n in range(GROUP)]
            values = along_rows(space_f[...], [held[r, :] for r in rows])
            values = [v - jnp.clip(v, -threshold, threshold) for v in values]
            values = along_rows(space_b[...], values)
            for n in range(GROUP):
                held[rows[n], :] = values[n]

    @pl.loop(0, last)
    def _(step):
        shrink(step)

        @pl.loop(0, WIN // GROUP)
        def _(group):
            forward(group, backward(group))

    shrink(last)

    @pl.loop(0, WIN // GROUP)
    def _(group):
        estimates = backward(group)
        for n in range(GROUP):
            line = group * GROUP + n
            start = pl.multiple_of(line * WIN, 8)
            weight = lines[pl.ds(line, 1), :]
            out[pl.ds(start, WIN), :] = estimates[n] * (plane[...] * weight)
            if n % PIECE == PIECE - 1:
                give(group * (GROUP // PIECE) + n // PIECE)


def reconstruct(windows, counts, levels):
    fixed = tables()
    shape = (WPD,) + windows.shape[1:]
    vmem = pl.BlockSpec(memory_space=pltpu.VMEM)
    smem = pl.BlockSpec(memory_space=pltpu.SMEM)
    hbm = pl.BlockSpec(memory_space=pl.ANY)
    return pl.pallas_call(
        shrink_kernel,
        in_specs=[smem, smem, hbm] + [vmem] * len(fixed),
        out_specs=[hbm, vmem],
        out_shape=[
            jax.ShapeDtypeStruct(shape, jnp.float32),
            jax.ShapeDtypeStruct((8, WIN_T), jnp.float32),
        ],
        scratch_shapes=[
            pltpu.VMEM((WIN * PITCH, WIN_T), jnp.float32),
            pltpu.VMEM(shape, jnp.float32),
            pltpu.VMEM(shape, jnp.float32),
            pltpu.SemaphoreType.DMA((WPD, CHUNKS)),
            pltpu.SemaphoreType.DMA((WPD, CHUNKS)),
        ],
        compiler_params=pltpu.CompilerParams(vmem_limit_bytes=40 * 2**20),
        name="shrink",
    )(counts, levels, windows, *fixed)


class Links:
    def __init__(self, sizes, send_sems, recv_sems):
        self.sizes, self.send_sems, self.recv_sems = sizes, send_sems, recv_sems
        self.me = {axis: lax.axis_index(axis) for axis in sizes}
        self.used = 0

    def has(self, axis, step):
        if step > 0:
            return self.me[axis] < self.sizes[axis] - 1
        return self.me[axis] > 0

    def greet(self):
        barrier = pltpu.get_barrier_semaphore()
        total = 0
        for axis in self.sizes:
            for step in (-1, 1):
                there = self.has(axis, step)
                total = total + there.astype(jnp.int32)

                @pl.when(there)
                def _():
                    pl.semaphore_signal(
                        barrier,
                        inc=1,
                        device_id={axis: self.me[axis] + step},
                        device_id_type=pl.DeviceIdType.MESH,
                    )

        return barrier, total

    def barrier(self):
        barrier, total = self.greet()
        pl.semaphore_wait(barrier, total)

    def copy(self, source, target, axis, index):
        number = self.used
        self.used += 1
        return pltpu.make_async_remote_copy(
            src_ref=source,
            dst_ref=target,
            send_sem=self.send_sems.at[number],
            recv_sem=self.recv_sems.at[number],
            device_id={axis: index},
            device_id_type=pl.DeviceIdType.MESH,
        )

    def send(self, source, target, axis, step):
        copy = self.copy(source, target, axis, self.me[axis] + step)

        @pl.when(self.has(axis, step))
        def _():
            copy.start()

        return copy, axis, step

    def arrive(self, sent, otherwise=None):
        copy, axis, step = sent
        there = self.has(axis, -step)

        @pl.when(there)
        def _():
            copy.wait_recv()

        if otherwise is not None:

            @pl.when(jnp.logical_not(there))
            def _():
                otherwise()

    def arrive_coded(self, sent, then, otherwise=None):
        _, axis, step = sent[0]
        there = self.has(axis, -step)

        @pl.when(there)
        def _():
            for copy, _, _ in sent:
                copy.wait_recv()
            then()

        if otherwise is not None:

            @pl.when(jnp.logical_not(there))
            def _():
                otherwise()

    def finish(self, sents):
        for copy, axis, step in sents:

            @pl.when(self.has(axis, step))
            def _():
                copy.wait_send()

    def partner(self, source, target):
        me = self.me["xl"]
        return self.copy(source, target, "xl", me + 1 - 2 * lax.rem(me, 2))


QUARTERS = WIN_T // HALO_T
UNIT = HALO // QUARTERS


def lane_numbers(shape):
    return lax.broadcasted_iota(jnp.int32, shape, len(shape) - 1)


def turned(value, shift):
    shift = shift % WIN_T
    return pltpu.roll(value, shift, value.ndim - 1) if shift else value


def pieces(parts):
    for h in range(parts):
        for q in range(QUARTERS):
            start = h * HALO + q * UNIT
            yield h, q, pl.ds(start, UNIT), pl.ds(h * UNIT, UNIT)


TOP = 32767


def encode(block, words, scale, gaps):
    values = block.reshape(-1, 8, WIN_T)
    if gaps:
        gone = values == DEAD
        values = jnp.where(gone, 0.0, values)
    most = jnp.maximum(jnp.max(jnp.abs(values), axis=0), 1e-30)
    codes = jnp.round(values * (TOP / most)[None]).astype(jnp.int32)
    if gaps:
        codes = jnp.where(gone, -TOP - 1, codes)
    half = codes.shape[0] // 2
    words[...] = codes[:half] * (2 * TOP + 2) + (codes[half:] + (TOP + 1))
    scale[...] = most * (1.0 / TOP)


def decode(words, scale, shape, gaps):
    packed = words[...]
    first = packed >> 16
    second = (packed & 0xFFFF) - (TOP + 1)
    codes = jnp.concatenate([first, second], axis=0)
    values = codes.astype(jnp.float32) * scale[...][None]
    if gaps:
        values = jnp.where(codes == -TOP - 1, DEAD, values)
    return values.reshape(shape)


def code_shapes(core_x):
    tiles = core_x // 8
    large, small = HALO * tiles // 2, UNIT * tiles // 2
    words = [(2, 2, n, 8, WIN_T) for n in (large, small, small)]
    return [pltpu.VMEM(w, jnp.int32) for w in words] + [
        pltpu.VMEM((2, 2, 3, 8, WIN_T), jnp.float32)
    ]


class Coder:
    def __init__(self, send, words, scales, gaps):
        self.send, self.words, self.scales, self.gaps = send, words, scales, gaps

    def put(self, block, kind, side):
        words, scale = self.words[kind], self.scales
        encode(block, words.at[0, side], scale.at[0, side, kind], self.gaps)

    def go(self, kind, side):
        words, scale = self.words[kind], self.scales
        step = 2 * side - 1
        return (
            self.send(words.at[0, side], words.at[1, side], "il", step),
            self.send(scale.at[0, side, kind], scale.at[1, side, kind], "il", step),
        )

    def get(self, kind, side, shape):
        words, scale = self.words[kind], self.scales
        return decode(words.at[1, side], scale.at[1, side, kind], shape, self.gaps)


def in_quarter(lanes, q):
    return (lanes >= q * HALO_T) & (lanes < (q + 1) * HALO_T)


def gather_kernel(
    sizes,
    traces,
    flags,
    out,
    mine,
    live,
    raw,
    early,
    late,
    to_next,
    to_prev,
    ready,
    words_raw,
    words_early,
    words_late,
    scales,
    local_sems,
    send_sems,
    recv_sems,
):
    links = Links(sizes, send_sems, recv_sems)
    core_i, core_x, _ = mine.shape
    own = pltpu.make_async_copy(traces, mine, local_sems.at[0])
    own.start()
    known = pltpu.make_async_copy(flags, live, local_sems.at[1])
    known.start()
    barrier, total = links.greet()
    known.wait()
    square = (core_x, core_x)
    same = lax.broadcasted_iota(jnp.int32, square, 0) == lax.broadcasted_iota(jnp.int32, square, 1)
    spread = [jnp.where(same, live[pl.ds(n, 1), :], 0) for n in range(core_i)]
    spread = jnp.concatenate(spread, axis=0).astype(jnp.float32).astype(jnp.bfloat16)
    ones = jnp.ones((core_x, WIN_T), jnp.bfloat16)
    seen = jnp.dot(spread, ones, preferred_element_type=jnp.float32).reshape(mine.shape)
    own.wait()
    mine[...] = jnp.where(seen > 0.5, mine[...], DEAD)
    inner_x = pl.ds(HALO, core_x)
    low_i, high_i = pl.ds(0, HALO), pl.ds(HALO + core_i, HALO)
    sent = []

    def send(*args):
        sent.append(links.send(*args))
        return sent[-1]

    coder = Coder(send, (words_raw, words_early, words_late), scales, True)
    coder.put(mine[pl.ds(0, HALO)], 0, 0)
    coder.put(mine[pl.ds(core_i - HALO, HALO)], 0, 1)
    pl.semaphore_wait(barrier, total)
    waits = [(coder.go(0, 0), raw, 0, 0, high_i), (coder.go(0, 1), raw, 0, 1, low_i)]

    for h, q, span, row in pieces(core_i // HALO):
        block = mine[span]
        lanes = lane_numbers(block.shape)
        chosen = in_quarter(lanes, q)
        first = turned(block, q * HALO_T)
        final = turned(block, q * HALO_T - (WIN_T - HALO_T))
        to_prev[row] = first if q == 0 else jnp.where(chosen, first, to_prev[row])
        to_next[row] = final if q == 0 else jnp.where(chosen, final, to_next[row])

    inner_p = pl.ds(UNIT, core_i // QUARTERS)
    early_in = send(to_next, early.at[inner_p, inner_x], "ta", 1)
    late_in = send(to_prev, late.at[inner_p, inner_x], "ta", -1)
    raw[pl.ds(HALO, core_i), inner_x] = mine[...]

    def blank(target, source):
        def fill():
            target[inner_p, inner_x] = jnp.where(source[...] == DEAD, DEAD, 0.0)

        return fill

    low_p, high_p = pl.ds(0, UNIT), pl.ds(UNIT + core_i // QUARTERS, UNIT)
    from_p = pl.ds(core_i // QUARTERS, UNIT)
    for arrival, buffer, source, kind in (
        (early_in, early, to_next, 1),
        (late_in, late, to_prev, 2),
    ):
        links.arrive(arrival, blank(buffer, source))
        coder.put(buffer[pl.ds(UNIT, UNIT), inner_x], kind, 0)
        coder.put(buffer[from_p, inner_x], kind, 1)
        waits += [
            (coder.go(kind, 0), buffer, kind, 0, high_p),
            (coder.go(kind, 1), buffer, kind, 1, low_p),
        ]

    def missing(target, first, second):
        def fill():
            shape = target.at[first, second].shape
            target[first, second] = jnp.full(shape, DEAD, jnp.float32)

        return fill

    def restored(target, kind, side, first):
        def fill():
            shape = target.at[first, inner_x].shape
            target[first, inner_x] = coder.get(kind, side, shape)

        return fill

    for arrival, buffer, kind, side, place in waits:
        links.arrive_coded(
            arrival, restored(buffer, kind, side, place), missing(buffer, place, inner_x)
        )

    waits = []
    low_x, high_x = pl.ds(0, HALO), pl.ds(HALO + core_x, HALO)
    for buffer in (raw, early, late):
        whole = pl.ds(0, buffer.shape[0])
        up = send(buffer.at[whole, pl.ds(core_x, HALO)], buffer.at[whole, low_x], "xl", 1)
        down = send(buffer.at[whole, pl.ds(HALO, HALO)], buffer.at[whole, high_x], "xl", -1)
        waits += [(up, buffer, low_x), (down, buffer, high_x)]

    def final_window(span, row, columns):
        block = raw[span, columns]
        lanes = lane_numbers(block.shape)
        shift = WIN_T - HALO_T - q * HALO_T
        added = turned(late[row, columns], shift)
        whole = jnp.where(lanes < WIN_T - HALO_T, turned(block, -HALO_T), added)
        ready[1, span, columns] = whole

    trades = []
    for h, q, span, row in pieces(WIN // HALO):
        final_window(span, row, inner_x)
        if q == QUARTERS - 1:
            part = pl.ds(h * HALO, HALO)
            trades.append(links.partner(ready.at[1, part, inner_x], out.at[2, part, inner_x]))
            trades[-1].start()
    for arrival, buffer, place in waits:
        links.arrive(arrival, missing(buffer, pl.ds(0, buffer.shape[0]), place))
    for columns in (low_x, high_x):
        for h, q, span, row in pieces(WIN // HALO):
            final_window(span, row, columns)
        trades.append(links.partner(ready.at[1, :, columns], out.at[2, :, columns]))
        trades[-1].start()

    keep = [pltpu.make_async_copy(ready.at[n], out.at[n], local_sems.at[n]) for n in range(WPD)]
    keep[1].start()
    for h, q, span, row in pieces(WIN // HALO):
        block = raw[span]
        lanes = lane_numbers(block.shape)
        added = turned(early[row], -q * HALO_T)
        ready[0, span] = jnp.where(lanes < HALO_T, added, turned(block, HALO_T))
    keep[0].start()
    keep[0].wait()
    keep[1].wait()
    for trade in trades:
        trade.wait()
    links.finish(sent)


def gather_windows(traces, live, sizes):
    packed = (WIN // QUARTERS, WIN, WIN_T)
    small = (traces.shape[0] // QUARTERS, traces.shape[1], WIN_T)
    scratch = [traces.shape, (WIN, WIN, WIN_T), packed, packed, small, small]
    scratch += [(WPD, WIN, WIN, WIN_T)]
    codes = code_shapes(traces.shape[1])
    return pl.pallas_call(
        functools.partial(gather_kernel, sizes),
        out_shape=jax.ShapeDtypeStruct((3, WIN, WIN, WIN_T), jnp.float32),
        in_specs=[
            pl.BlockSpec(memory_space=pltpu.HBM),
            pl.BlockSpec(memory_space=pltpu.HBM),
        ],
        out_specs=pl.BlockSpec(memory_space=pl.ANY),
        scratch_shapes=[pltpu.VMEM(traces.shape, jnp.float32), pltpu.VMEM(live.shape, jnp.int32)]
        + [pltpu.VMEM(shape, jnp.float32) for shape in scratch[1:]]
        + codes
        + [pltpu.SemaphoreType.DMA((n,)) for n in (WPD, 28, 28)],
        compiler_params=pltpu.CompilerParams(
            collective_id=0, has_side_effects=True, vmem_limit_bytes=40 * 2**20
        ),
        name="gather_windows",
    )(traces, live)


def scatter_kernel(
    sizes,
    flag,
    results,
    out,
    done,
    foreign,
    raw,
    early,
    late,
    side_raw,
    side_early,
    side_late,
    words_raw,
    words_early,
    words_late,
    scales,
    from_time,
    local_sems,
    send_sems,
    recv_sems,
):
    links = Links(sizes, send_sems, recv_sems)
    loads = [
        pltpu.make_async_copy(results.at[n], done.at[n], local_sems.at[n]) for n in range(WPD)
    ]
    for load in loads:
        load.start()
    links.barrier()
    core_i, core_x, _ = out.shape
    inner_x = pl.ds(HALO, core_x)
    sent = []

    def send(*args):
        sent.append(links.send(*args))
        return sent[-1]

    parts = [pl.ds(h * HALO, HALO) for h in range(WIN // HALO)]
    trades = [links.partner(results.at[1, part], foreign.at[part]) for part in parts]
    for trade in trades:
        trade.start()
    for load in loads:
        load.wait()
    for h, q, span, row in pieces(WIN // HALO):
        block = done[0, span]
        lanes = lane_numbers(block.shape)
        raw[span] = jnp.where(lanes < WIN_T - HALO_T, turned(block, -HALO_T), 0.0)
        first = turned(block, q * HALO_T)
        early[row] = first if q == 0 else jnp.where(in_quarter(lanes, q), first, early[row])
    for h, q, span, row in pieces(WIN // HALO):
        if q == 0:
            trades[h].wait()
        block = jnp.where(flag[...][None, :1, :] > 0.5, foreign[span], done[1, span])
        lanes = lane_numbers(block.shape)
        raw[span] = raw[span] + jnp.where(lanes >= HALO_T, turned(block, HALO_T), 0.0)
        final = turned(block, q * HALO_T - (WIN_T - HALO_T))
        late[row] = final if q == 0 else jnp.where(in_quarter(lanes, q), final, late[row])

    def add(target, first, second, source):
        there = target[first, second]
        target[first, second] = there + source[...]

    waits = []
    for buffer, side in ((raw, side_raw), (early, side_early), (late, side_late)):
        whole = pl.ds(0, buffer.shape[0])
        down = send(buffer.at[whole, pl.ds(0, HALO)], side.at[0], "xl", -1)
        up = send(buffer.at[whole, pl.ds(HALO + core_x, HALO)], side.at[1], "xl", 1)
        waits += [
            (down, buffer, whole, pl.ds(core_x, HALO), side.at[0]),
            (up, buffer, whole, pl.ds(HALO, HALO), side.at[1]),
        ]

    def gathered(waits):
        for arrival, buffer, first, second, source in waits:
            links.arrive(arrival)
            _, axis, step = arrival

            @pl.when(links.has(axis, -step))
            def _():
                add(buffer, first, second, source)

    gathered(waits)

    coder = Coder(send, (words_raw, words_early, words_late), scales, False)
    waits = []
    for buffer, kind, width in ((early, 1, UNIT), (late, 2, UNIT), (raw, 0, HALO)):
        total = buffer.shape[0]
        inner = total - 2 * width
        coder.put(buffer[pl.ds(0, width), inner_x], kind, 0)
        coder.put(buffer[pl.ds(total - width, width), inner_x], kind, 1)
        waits += [
            (coder.go(kind, 0), buffer, kind, 0, pl.ds(inner, width)),
            (coder.go(kind, 1), buffer, kind, 1, pl.ds(width, width)),
        ]

    def added(target, kind, side, first):
        def fill():
            there = target[first, inner_x]
            target[first, inner_x] = there + coder.get(kind, side, there.shape)

        return fill

    for arrival, buffer, kind, side, place in waits[:4]:
        links.arrive_coded(arrival, added(buffer, kind, side, place))
    inner_p = pl.ds(UNIT, core_i // QUARTERS)
    back = send(early.at[inner_p, inner_x], from_time.at[0], "ta", -1)
    ahead = send(late.at[inner_p, inner_x], from_time.at[1], "ta", 1)
    for arrival, buffer, kind, side, place in waits[4:]:
        links.arrive_coded(arrival, added(buffer, kind, side, place))
    out[...] = raw[pl.ds(HALO, core_i), inner_x]
    for arrival, side, shift in ((back, 0, WIN_T - HALO_T), (ahead, 1, 0)):
        links.arrive(arrival)
        _, axis, step = arrival

        @pl.when(links.has(axis, -step))
        def _():
            for h, q, span, row in pieces(core_i // HALO):
                block = turned(from_time[side, row], shift - q * HALO_T)
                lanes = lane_numbers(block.shape)
                kept = in_quarter(lanes, shift // HALO_T)
                out[span] = out[span] + jnp.where(kept, block, 0.0)

    links.finish(sent)


def scatter_windows(flag, done, shape, sizes):
    core_i, core_x, _ = shape
    packed = (WIN // QUARTERS, WIN, WIN_T)
    small = (WIN // QUARTERS, HALO, WIN_T)
    scratch = [
        (WPD, WIN, WIN, WIN_T),
        (WIN, WIN, WIN_T),
        (WIN, WIN, WIN_T),
        packed,
        packed,
        (2, WIN, HALO, WIN_T),
        (2,) + small,
        (2,) + small,
    ]
    time_side = pltpu.VMEM((2, core_i // QUARTERS, core_x, WIN_T), jnp.float32)
    codes = code_shapes(core_x) + [time_side]
    return pl.pallas_call(
        functools.partial(scatter_kernel, sizes),
        out_shape=jax.ShapeDtypeStruct(shape, jnp.float32),
        in_specs=[pl.BlockSpec(memory_space=pltpu.VMEM), pl.BlockSpec(memory_space=pl.ANY)],
        out_specs=pl.BlockSpec(memory_space=pltpu.VMEM),
        scratch_shapes=[pltpu.VMEM(shape, jnp.float32) for shape in scratch]
        + codes
        + [pltpu.SemaphoreType.DMA((n,)) for n in (WPD, 28, 28)],
        compiler_params=pltpu.CompilerParams(
            collective_id=1, has_side_effects=True, vmem_limit_bytes=40 * 2**20
        ),
        name="scatter_windows",
    )(flag, done)


def shards(sizes, traces, live, counts, levels):
    windows = gather_windows(traces, live, sizes).reshape(3, WIN * WIN, WIN_T)
    done, flag = reconstruct(windows, counts, levels)
    return scatter_windows(flag, done.reshape(WPD, WIN, WIN, WIN_T), traces.shape, sizes)


def solution(mesh):
    placed = (P("il", "xl", "ta"), P("il", "xl"), P("il", None, "ta"), P())
    sizes = {axis: mesh.shape[axis] for axis in ("il", "xl", "ta")}
    return jax.shard_map(
        functools.partial(shards, sizes),
        mesh=mesh,
        in_specs=placed,
        out_specs=P("il", "xl", "ta"),
        check_vma=False,
    )
```
